32 devices in a mesh: dp: 8 (over z, x), tile: 4 (over y, core).
Axes of the slice: x: 2, y: 2, z: 4, core: 2. Of those that a mesh axis runs over, the one named last changes fastest.
Arguments:
- features: bfloat16 [8, 8, 8, 8, 1584], P('dp', 'tile'), may hold values from -6 to 6
- cotangent: bfloat16 [8, 8, 8, 8, 1584], P('dp', 'tile'), may hold values from -6 to 6
- conv_weight: bfloat16 [29408, 128], P('dp'), may hold values from -0.125 to 0.125
- squeeze_weight: bfloat16 [1584, 363], replicated, may hold values from -0.15625 to 0.15625
- excite_weight: bfloat16 [363, 1584], replicated, may hold values from -0.3125 to 0.3125
- live_count: int32 [8, 4], P('dp', 'tile'), may hold values from 1 to 2, as said below
- neighbours: int32 [8, 8, 8], P('dp', 'tile'), may hold values from -1 to 7, as said below
Outputs:
- output: bfloat16 [8, 8, 8, 8, 1584], P('dp', 'tile')
- grad_features: bfloat16 [8, 8, 8, 8, 1584], P('dp', 'tile')
- grad_conv: float32 [29408, 128], P('dp')
- grad_squeeze: float32 [1584, 363], replicated
- grad_excite: float32 [363, 1584], replicated
The draws below stay inside these ranges and needn't reach their ends.
Inputs may be any that keep to these rules, and one draw needn't show every extreme that they name: `live_count`: the tiles with tissue on a device fill its first slots; in every slide some device has all 2 slots filled. `neighbours`: an entry is -1 or the index of a tile with tissue of the same slide (device index times 2 plus slot); a slot without tissue lists only -1.
All inputs are finite; a program needn't handle non-finite values.
Results may differ from the reference program's by a relative error of at most 0.006.
Values may be sent and summed in bfloat16 or wider, within the bound.
No kernel may reach another device: no remote copies, remote signals or barrier semaphores. Data moves between devices by JAX's collectives and lax.ppermute only.
A program may use at most 128 MiB of HBM per device.

```python
import jax
import jax.numpy as jnp
from jax import lax

CG = 264
GROUPS = 6
SE = 363
P_SIZE = 8
SLOTS = 2
CH = 1584
TILES = 8
SLIDES = 8
WROWS = 29408


def tissue_counts(key):
    devices_per = TILES // SLOTS
    first = jax.random.randint(jax.random.fold_in(key, 11), (SLIDES, devices_per), 1, SLOTS + 1)
    second = jax.random.randint(jax.random.fold_in(key, 13), (SLIDES, devices_per), 1, SLOTS + 1)
    counts = jnp.minimum(first, second)
    fullest = jnp.arange(SLIDES)[:, None] % devices_per == jnp.arange(devices_per)[None, :]
    return jnp.where(fullest, SLOTS, counts).astype(jnp.int32)


def draw_live_count(key, part):
    return tissue_counts(key)


def draw_neighbours(key, part):
    devices_per = TILES // SLOTS
    counts = tissue_counts(key)
    ends = jnp.cumsum(counts, axis=1).astype(jnp.int32)
    starts = ends - counts
    totals = ends[:, -1]
    raw = jax.random.randint(jax.random.fold_in(key, 17), (SLIDES, TILES, 8), 0, 1 << 30)
    picks = raw % totals[:, None, None]
    owner = jnp.sum((picks[..., None] >= ends[:, None, None, :]).astype(jnp.int32), axis=-1).astype(jnp.int32)
    chosen = owner[..., None] == jnp.arange(devices_per)[None, None, None, :]
    begin = jnp.sum(jnp.where(chosen, starts[:, None, None, :], 0), axis=-1).astype(jnp.int32)
    target = owner * SLOTS + picks - begin
    absent = jax.random.randint(jax.random.fold_in(key, 19), (SLIDES, TILES, 8), 0, 4) == 0
    own_dev = jnp.arange(TILES) // SLOTS
    own_slot = jnp.arange(TILES) % SLOTS
    own_live = own_slot[None, :] < jnp.take(counts, own_dev, axis=1)
    keep = jnp.logical_and(jnp.logical_not(absent), own_live[:, :, None])
    return jnp.where(keep, target, -1).astype(jnp.int32)


def level_of(key, shape, cuts, smallest, largest):
    gain, own = 1.0, jax.random.fold_in(key, 6)
    for position, blocks in cuts:
        draws = jnp.exp(jax.random.uniform(jax.random.fold_in(own, position), (blocks,), jnp.float32, smallest / len(cuts), largest / len(cuts)))
        gain = gain * jnp.repeat(draws, shape[position] // blocks).reshape([-1 if axis == position else 1 for axis in range(len(shape))])
    return gain


def noise(key, extent, scale, limit, pieces=(), dtype=jnp.bfloat16):
    array = jax.random.normal(key, extent, jnp.float32) * scale
    if len(pieces) > 0:
        array = level_of(key, extent, pieces, -0.22, 0.18) * array
    return jnp.clip(array, min=-limit, max=limit).astype(dtype)


def setup_inputs(seed: int = 0) -> dict:
    seeds = jax.random.split(jax.random.key(seed), 8)
    return {
        "features": noise(seeds[0], (SLIDES, TILES, P_SIZE, P_SIZE, CH), 1.0, 6.0, ((0, 8), (1, 4))),
        "cotangent": noise(seeds[1], (SLIDES, TILES, P_SIZE, P_SIZE, CH), 1.0, 6.0, ((0, 8), (1, 4))),
        "conv_weight": noise(seeds[2], (WROWS, 128), (9 * CG) ** -0.5, 0.125, ((0, 8),)),
        "squeeze_weight": noise(seeds[3], (CH, SE), CH ** -0.5, 0.15625),
        "excite_weight": noise(seeds[4], (SE, CH), SE ** -0.5, 0.3125),
        "live_count": draw_live_count(jax.random.fold_in(seeds[7], 71), 0),
        "neighbours": draw_neighbours(jax.random.fold_in(seeds[7], 71), 0),
    }


def make_strips(tile_data):
    return jnp.stack([tile_data[:, 0], tile_data[:, -1], tile_data[:, :, 0], tile_data[:, :, -1]], axis=1)


def fetch_rim(piece_all, safe_ids, present, offset):
    fetched = jnp.take(piece_all, safe_ids[:, offset], axis=0)
    keep_row = present[:, offset].reshape((-1,) + (1,) * (fetched.ndim - 1))
    return jnp.where(keep_row, fetched, jnp.zeros_like(fetched))


def pad_tiles(tile_data, strips, neighbor_ids):
    last_pos = tile_data.shape[1] - 1
    present = neighbor_ids >= 0
    safe_ids = jnp.maximum(neighbor_ids, 0)
    corner_tl = fetch_rim(strips[:, 1, last_pos], safe_ids, present, 0)
    top_row = fetch_rim(strips[:, 1], safe_ids, present, 1)
    corner_tr = fetch_rim(strips[:, 1, 0], safe_ids, present, 2)
    left_col = fetch_rim(strips[:, 3], safe_ids, present, 3)
    right_col = fetch_rim(strips[:, 2], safe_ids, present, 4)
    corner_bl = fetch_rim(strips[:, 0, last_pos], safe_ids, present, 5)
    bottom_row = fetch_rim(strips[:, 0], safe_ids, present, 6)
    corner_br = fetch_rim(strips[:, 0, 0], safe_ids, present, 7)
    upper = jnp.concatenate([corner_tl[:, None], top_row, corner_tr[:, None]], axis=1)
    lower = jnp.concatenate([corner_bl[:, None], bottom_row, corner_br[:, None]], axis=1)
    middle = jnp.concatenate([left_col[:, :, None], tile_data, right_col[:, :, None]], axis=2)
    return jnp.concatenate([upper[:, None], middle, lower[:, None]], axis=1)


def unfold(padded):
    edge_len = padded.shape[1] - 2
    parts = [padded[:, row_off:row_off + edge_len, col_off:col_off + edge_len] for row_off in range(3) for col_off in range(3)]
    return jnp.stack(parts, axis=3).reshape(-1, 9, padded.shape[-1])


def fold_back(col_grads, slot_num, edge_len):
    shaped = col_grads.reshape(slot_num, edge_len, edge_len, 9, col_grads.shape[-1])
    grad_pad = jnp.zeros((slot_num, edge_len + 2, edge_len + 2, col_grads.shape[-1]), jnp.float32)
    for tap_pos in range(9):
        row_off, col_off = divmod(tap_pos, 3)
        grad_pad = grad_pad.at[:, row_off:row_off + edge_len, col_off:col_off + edge_len].add(shaped[:, :, :, tap_pos])
    return grad_pad


def border_pieces(grad_pad):
    edges = jnp.stack([grad_pad[:, 0, 1:-1], grad_pad[:, 1:-1, 0], grad_pad[:, 1:-1, -1], grad_pad[:, -1, 1:-1]], axis=1)
    corners = jnp.stack([grad_pad[:, 0, 0], grad_pad[:, 0, -1], grad_pad[:, -1, 0], grad_pad[:, -1, -1]], axis=1)
    return edges.astype(jnp.bfloat16), corners.astype(jnp.bfloat16)


def border_in(edges_all, corners_all, ids_all, own_ids, edge_len):
    matches = (ids_all[None, :, :] == own_ids[:, None, None]).astype(jnp.float32)
    edges_f = edges_all.astype(jnp.float32)
    corners_f = corners_all.astype(jnp.float32)
    high = lax.Precision.HIGHEST

    def spread_edge(offset, member):
        return jnp.einsum('st,tpc->spc', matches[:, :, offset], edges_f[:, member], precision=high)

    def spread_corner(offset, member):
        return jnp.einsum('st,tc->sc', matches[:, :, offset], corners_f[:, member], precision=high)

    last_pos = edge_len - 1
    incoming = jnp.zeros((own_ids.shape[0], edge_len, edge_len, edges_all.shape[-1]), jnp.float32)
    incoming = incoming.at[:, last_pos, :].add(spread_edge(1, 0))
    incoming = incoming.at[:, :, last_pos].add(spread_edge(3, 1))
    incoming = incoming.at[:, :, 0].add(spread_edge(4, 2))
    incoming = incoming.at[:, 0, :].add(spread_edge(6, 3))
    incoming = incoming.at[:, last_pos, last_pos].add(spread_corner(0, 0))
    incoming = incoming.at[:, last_pos, 0].add(spread_corner(2, 1))
    incoming = incoming.at[:, 0, last_pos].add(spread_corner(5, 2))
    incoming = incoming.at[:, 0, 0].add(spread_corner(7, 3))
    return incoming


def dsilu(value):
    sig = jax.nn.sigmoid(value)
    return sig * (1.0 + value * (1.0 - sig))


def reference(features, cotangent, conv_weight, squeeze_weight, excite_weight, live_count, neighbours):
    high = lax.Precision.HIGHEST
    kernel = conv_weight.reshape(-1)[:GROUPS * 9 * CG * CG].reshape(GROUPS, 9, CG, CG).astype(jnp.float32)
    w_squeeze = squeeze_weight.astype(jnp.float32)
    w_excite = excite_weight.astype(jnp.float32)
    edge_len = P_SIZE

    def slide_pass(carry, inputs):
        tile_data, cot_data, counts, neighbor_ids = inputs
        live = ((jnp.arange(TILES) % SLOTS) < jnp.repeat(counts, SLOTS)).astype(jnp.float32)
        tile_mask = live[:, None, None, None]
        padded = pad_tiles(tile_data, make_strips(tile_data), neighbor_ids)
        patches = unfold(padded).astype(jnp.float32).reshape(-1, 9, GROUPS, CG)
        hidden = jnp.einsum('rkgi,gkio->rgo', patches, kernel, precision=high).reshape(TILES, edge_len, edge_len, CH)
        active = (jax.nn.silu(hidden) * tile_mask).astype(jnp.bfloat16)
        active_f = active.astype(jnp.float32)
        pixel_total = jnp.sum(counts).astype(jnp.float32) * (edge_len * edge_len)
        pooled = jnp.sum(active_f, axis=(0, 1, 2)) / pixel_total
        squeeze_pre = jnp.dot(pooled, w_squeeze, precision=high)
        squeezed = jax.nn.silu(squeeze_pre)
        excite = jax.nn.sigmoid(jnp.dot(squeezed, w_excite, precision=high))
        output = ((tile_data.astype(jnp.float32) + active_f * excite) * tile_mask).astype(jnp.bfloat16)
        cot_live = cot_data.astype(jnp.float32) * tile_mask
        gate_grad = jnp.sum(cot_live * active_f, axis=(0, 1, 2))
        excite_pre_grad = gate_grad * excite * (1.0 - excite)
        squeeze_pre_grad = jnp.dot(excite_pre_grad, w_excite.T, precision=high) * dsilu(squeeze_pre)
        pool_grad = jnp.dot(squeeze_pre_grad, w_squeeze.T, precision=high)
        hidden_grad = ((cot_live * excite + pool_grad / pixel_total) * dsilu(hidden) * tile_mask).astype(jnp.bfloat16)
        grad_rows = hidden_grad.astype(jnp.float32).reshape(-1, GROUPS, CG)
        col_grads = jnp.einsum('rgo,gkio->rkgi', grad_rows, kernel, precision=high).reshape(-1, 9, CH)
        grad_pad = fold_back(col_grads, TILES, edge_len)
        grad_w = jnp.einsum('rkgi,rgo->gkio', patches, grad_rows, precision=high)
        edges, corners = border_pieces(grad_pad)
        incoming = border_in(edges, corners, neighbor_ids, jnp.arange(TILES), edge_len)
        grad_in = ((cot_data.astype(jnp.float32) + grad_pad[:, 1:-1, 1:-1] + incoming) * tile_mask).astype(jnp.bfloat16)
        return carry + grad_w, (output, grad_in, pooled, squeeze_pre_grad, squeezed, excite_pre_grad)

    start = jnp.zeros((GROUPS, 9, CG, CG), jnp.float32)
    grad_w, stacked = lax.scan(slide_pass, start, (features, cotangent, live_count, neighbours))
    output, grad_features, pooled_all, squeeze_all, squeezed_all, excite_all = stacked
    grad_squeeze = jnp.dot(pooled_all.T, squeeze_all, precision=high)
    grad_excite = jnp.dot(squeezed_all.T, excite_all, precision=high)
    flat_grad = grad_w.reshape(-1)
    grad_conv = jnp.pad(flat_grad, (0, WROWS * 128 - flat_grad.shape[0])).reshape(WROWS, 128)
    return (output, grad_features, grad_conv, grad_squeeze, grad_excite)
```

```python
import functools

import jax
import jax.numpy as jnp
from jax import lax
from jax.experimental import pallas as pl
from jax.experimental.pallas import tpu as pltpu
from jax.sharding import Mesh, PartitionSpec as P

CG = 264
HALF = 3 * CG
TAPROWS = 27 * CG
LEAD = 33 * (TAPROWS // 16)
CH = 2 * HALF
F32 = jnp.float32
BF16 = jnp.bfloat16
SWAP = [(0, 1), (1, 0)]
PCH = 64
NCH = 7
OROWS = 16 * PCH * NCH + 8
VMEM = pl.BlockSpec(memory_space=pltpu.VMEM)
SMEM = pl.BlockSpec(memory_space=pltpu.SMEM)
HBM = pl.BlockSpec(memory_space=pl.ANY)


def params():
    return pltpu.CompilerParams(vmem_limit_bytes=56 * 1024 * 1024)


def swap(value, axis):
    return lax.ppermute(value, axis, SWAP)


class Sizes:
    def __init__(self, rows, dl_num):
        self.rows = rows
        self.dl_num = dl_num
        self.bound = rows * dl_num - LEAD
        self.top = -(-self.bound // 16) * 16
        self.half = -(-rows // 64) * 32
        self.second = rows - self.half
        self.quarter = self.half // 2
        self.piece = -(-(self.quarter + self.top) // 48) * 48
        self.flat = self.top + 33 * PCH * NCH + 8


def split_body(sc, x_ref, mine_ref, send_ref):
    low = sc[0] == 0
    for slot in range(2):
        x = x_ref[64 * slot : 64 * slot + 64, :]
        x = jnp.where(slot < sc[4], x, jnp.zeros_like(x))
        first, second = x[:, :HALF], x[:, HALF:]
        mine_ref[slot] = jnp.where(low, first, second)
        send_ref[slot] = jnp.where(low, second, first)


def split_halves(sc, x):
    shape = jax.ShapeDtypeStruct((2, 64, HALF), BF16)
    return pl.pallas_call(
        split_body,
        out_shape=(shape, shape),
        in_specs=[SMEM, VMEM],
        out_specs=(VMEM, VMEM),
        compiler_params=params(),
        name="split_halves",
    )(sc, x)


def join_body(sc, a_ref, b_ref, out_ref, wide):
    low = sc[0] == 0
    for slot in range(2):
        a = a_ref[slot].astype(F32)
        b = b_ref[slot].astype(F32)
        live = slot < sc[4]
        first = jnp.where(low, a, b)
        second = jnp.where(low, b, a)
        wide[:, :HALF] = jnp.where(live, first, 0.0)
        wide[:, HALF:] = jnp.where(live, second, 0.0)
        out_ref[64 * slot : 64 * slot + 64, :] = wide[...].astype(BF16)


def join_halves(sc, a, b):
    return pl.pallas_call(
        join_body,
        out_shape=jax.ShapeDtypeStruct((128, CH), BF16),
        in_specs=[SMEM, VMEM, VMEM],
        out_specs=VMEM,
        scratch_shapes=[pltpu.VMEM((64, CH), F32)],
        compiler_params=params(),
        name="join_halves",
    )(sc, a, b)


def strips_body(own_ref, other_ref, out_ref):
    for t in range(4):
        ref = own_ref if t < 2 else other_ref
        x = ref[t % 2].astype(F32)
        cube = x.reshape(8, 8, HALF)
        out = jnp.concatenate([x[:8], x[56:], cube[:, 0, :], cube[:, 7, :]], axis=0)
        out_ref[t] = out.astype(BF16)


def make_strips(own, other):
    return pl.pallas_call(
        strips_body,
        out_shape=jax.ShapeDtypeStruct((4, 32, HALF), BF16),
        in_specs=[VMEM, VMEM],
        out_specs=VMEM,
        compiler_params=params(),
        name="make_strips",
    )(own, other)


def pad_body(sc, ids, own_ref, other_ref, s0, s1, s2, s3, x3_ref, strips, pad):
    for rel, ref in enumerate((s0, s1, s2, s3)):
        strips[rel] = ref[...]
    for t in range(4):
        ref = own_ref if t < 2 else other_ref
        x = ref[t % 2].astype(F32)
        for i in range(8):
            pad[1 + i, t, 1:9, :] = x[8 * i : 8 * i + 8]

        def piece(offset, member):
            n = ids[t, offset]
            safe = jnp.maximum(n, 0)
            rel = jnp.bitwise_xor(lax.shift_right_logical(safe, 1), sc[5])
            other = 2 * (t // 2) + jnp.bitwise_and(safe, 1)
            got = strips[rel, other].astype(F32)[8 * member : 8 * member + 8]
            return jnp.where(n >= 0, got, 0.0)

        pad[0, t, 0:1, :] = piece(0, 1)[7:8]
        pad[0, t, 1:9, :] = piece(1, 1)
        pad[0, t, 9:10, :] = piece(2, 1)[0:1]
        left = piece(3, 3)
        right = piece(4, 2)
        for i in range(8):
            pad[1 + i, t, 0:1, :] = left[i : i + 1]
            pad[1 + i, t, 9:10, :] = right[i : i + 1]
        pad[9, t, 0:1, :] = piece(5, 0)[7:8]
        pad[9, t, 1:9, :] = piece(6, 0)
        pad[9, t, 9:10, :] = piece(7, 0)[0:1]
    for i in range(10):
        for dx in range(3):
            row = pad[i, :, dx : dx + 8, :].reshape(32, HALF)
            for g in range(3):
                x3_ref[g, dx, i] = row[:, CG * g : CG * g + CG].astype(BF16)


def pad_tiles(sc, ids, own, other, strips):
    return pl.pallas_call(
        pad_body,
        out_shape=jax.ShapeDtypeStruct((3, 3, 10, 32, CG), BF16),
        in_specs=[SMEM, SMEM] + [VMEM] * 6,
        out_specs=VMEM,
        scratch_shapes=[
            pltpu.VMEM((4, 4, 32, HALF), BF16),
            pltpu.VMEM((10, 4, 16, HALF), F32),
        ],
        compiler_params=params(),
        name="pad_tiles",
    )(sc, ids, own, other, *strips)


def regroup_body(own_ref, other_ref, out_ref):
    x = [(own_ref if t < 2 else other_ref)[t % 2].astype(F32) for t in range(4)]
    for i in range(8):
        row = jnp.concatenate([x[t][8 * i : 8 * i + 8] for t in range(4)], axis=0)
        for g in range(3):
            out_ref[g, 32 * i : 32 * i + 32, :] = row[:, CG * g : CG * g + CG].astype(BF16)


def regroup(own, other):
    return pl.pallas_call(
        regroup_body,
        out_shape=jax.ShapeDtypeStruct((3, 256, CG), BF16),
        in_specs=[VMEM, VMEM],
        out_specs=VMEM,
        compiler_params=params(),
        name="regroup",
    )(own, other)


def weight_body(sizes, plan, sc, *refs):
    count = len(plan)
    srcs = refs[: count]
    bnd_ref, w_ref, land, flat, o0, o1, o2, sems = refs[count:]
    copies = []
    for pos, (rel, slot) in enumerate(plan):
        if rel is None:
            dst = land.at[:, slot]
        else:
            part = jnp.bitwise_xor(sc[2], slot[1]) if isinstance(slot, tuple) else slot
            dl = jnp.bitwise_xor(sc[1], rel)
            dst = land.at[dl, part]
            if isinstance(slot, tuple) and slot[0] is not None:
                dst = land.at[dl, part, pl.ds(slot[0] * sizes.quarter, sizes.quarter)]
        copies.append(pltpu.make_async_copy(srcs[pos], dst, sems.at[pos]))
        copies[-1].start()
    flat[: sizes.top, :] = bnd_ref[...].astype(F32)
    for copy in copies:
        copy.wait()
    for dl in range(sizes.dl_num):
        start = sizes.top + sizes.rows * dl
        flat[start : start + sizes.half, :] = land[dl, 0].astype(F32)
        start += sizes.second
        flat[start : start + sizes.half, :] = land[dl, 1].astype(F32)
    base = jnp.where(sc[0] == 0, sizes.top, sizes.top - sizes.bound)

    @pl.loop(0, NCH)
    def _(ch):
        start = base + ch * (33 * PCH)
        for k in range(16):
            rows = [flat[pl.ds(start + 2 * k + j, PCH, stride=33), :] for j in range(3)]
            x = jnp.concatenate(rows, axis=1)
            if k:
                x = pltpu.roll(x, 384 - 8 * k, axis=1)
            for col, ref in enumerate((o0, o1, o2)):
                ref[pl.ds(ch * (16 * PCH) + k, PCH, stride=16), :] = x[:, 128 * col : 128 * col + 128]

    off = jnp.where(sc[0] == 0, 0, 8)
    for g in range(3):
        for tap in range(9):
            here = pl.ds(pl.multiple_of(off + CG * (9 * g + tap), 8), CG)
            w_ref[g, tap, :, :128] = o0[here, :].astype(BF16)
            w_ref[g, tap, :, 128:256] = o1[here, :].astype(BF16)
            w_ref[g, tap, :, 256:] = o2[here, :8].astype(BF16)


def unpack_weight(sizes, sc, plan, arrays, bnd):
    return pl.pallas_call(
        functools.partial(weight_body, sizes, plan),
        out_shape=jax.ShapeDtypeStruct((3, 9, CG, CG), BF16),
        in_specs=[SMEM] + [HBM] * len(plan) + [VMEM],
        out_specs=VMEM,
        scratch_shapes=[
            pltpu.VMEM((sizes.dl_num, 2, sizes.half, 128), BF16),
            pltpu.VMEM((sizes.flat, 128), F32),
            pltpu.VMEM((OROWS, 128), F32),
            pltpu.VMEM((OROWS, 128), F32),
            pltpu.VMEM((OROWS, 128), F32),
            pltpu.SemaphoreType.DMA((len(plan),)),
        ],
        compiler_params=params(),
        name="unpack_weight",
    )(sc, *arrays, bnd)


def forward_body(sc, x3_ref, cot_ref, w_ref, hid_ref, sums_ref):
    acc = jnp.zeros((256, CG), F32)
    for dx in range(3):
        for dy in range(3):
            x = x3_ref[0, dx, dy : dy + 8].reshape(256, CG)
            acc += jnp.dot(x, w_ref[0, 3 * dy + dx], preferred_element_type=F32)
    hid_ref[0] = acc
    active = (acc * jax.nn.sigmoid(acc)).astype(BF16).astype(F32)
    gate = active * cot_ref[0].astype(F32)
    act4 = active.reshape(8, 4, 8, CG)
    gate4 = gate.reshape(8, 4, 8, CG)
    sums_ref[0] = jnp.full((8, CG), sc[4].astype(F32), F32)
    for row, (value, slide) in enumerate(((act4, 0), (act4, 1), (gate4, 0), (gate4, 1))):
        part = value[:, 2 * slide] + value[:, 2 * slide + 1]
        sums_ref[0, row : row + 1, :] = jnp.sum(jnp.sum(part, axis=0), axis=0, keepdims=True)


def forward(sc, x3, cot, w):
    return pl.pallas_call(
        forward_body,
        grid=(3,),
        out_shape=(
            jax.ShapeDtypeStruct((3, 256, CG), F32),
            jax.ShapeDtypeStruct((3, 8, CG), F32),
        ),
        in_specs=[
            SMEM,
            pl.BlockSpec((1, 3, 10, 32, CG), lambda g: (g, 0, 0, 0, 0)),
            pl.BlockSpec((1, 256, CG), lambda g: (g, 0, 0)),
            pl.BlockSpec((1, 9, CG, CG), lambda g: (g, 0, 0, 0)),
        ],
        out_specs=(
            pl.BlockSpec((1, 256, CG), lambda g: (g, 0, 0)),
            pl.BlockSpec((1, 8, CG), lambda g: (g, 0, 0)),
        ),
        compiler_params=params(),
        name="forward_conv",
    )(sc, x3, cot, w)


def thirds(x):
    hi = x.astype(BF16).astype(F32)
    mid = (x - hi).astype(BF16).astype(F32)
    low = (x - hi - mid).astype(BF16).astype(F32)
    return hi, mid, low


def exact_dot(x, w, contract):
    parts = jnp.concatenate([*thirds(x), jnp.zeros((10, x.shape[1]), F32)], axis=0).astype(BF16)
    out = lax.dot_general(parts, w, (((1,), (contract,)), ((), ())), preferred_element_type=F32)
    return out[0:2] + out[2:4] + out[4:6]


def gate_body(sc, mine_ref, other_ref, sq_ref, ex_ref, gate_ref, fin_ref, wide):
    low = sc[0] == 0
    for g in range(3):
        a = mine_ref[g]
        b = other_ref[g]
        a = a[0:4]
        b = jnp.concatenate([b[1:2], b[0:1], b[3:4], b[2:3]], axis=0)
        wide[0:4, CG * g : CG * g + CG] = jnp.where(low, a, b)
        wide[0:4, HALF + CG * g : HALF + CG * g + CG] = jnp.where(low, b, a)
    counts = jnp.concatenate([mine_ref[0][4:5, 0:1], other_ref[0][4:5, 0:1]], axis=0)
    total = counts * 64.0
    pooled = wide[0:2, :] / total
    gate = wide[2:4, :]
    w_squeeze = sq_ref[...]
    w_excite = ex_ref[...]
    pre = exact_dot(pooled, w_squeeze, 0)
    sig = jax.nn.sigmoid(pre)
    squeezed = pre * sig
    excite = jax.nn.sigmoid(exact_dot(squeezed, w_excite, 0))
    excite_grad = gate * excite * (1.0 - excite)
    slope = sig * (1.0 + pre * (1.0 - sig))
    squeeze_grad = exact_dot(excite_grad, w_excite, 1) * slope
    pool = exact_dot(squeeze_grad, w_squeeze, 1) / total
    half_e = jnp.where(low, excite[:, :HALF], excite[:, HALF:])
    half_p = jnp.where(low, pool[:, :HALF], pool[:, HALF:])
    for g in range(3):
        gate_ref[g, 0:2, :] = half_e[:, CG * g : CG * g + CG]
        gate_ref[g, 2:4, :] = half_p[:, CG * g : CG * g + CG]

    def ordered(x):
        return jnp.where(low, x, jnp.concatenate([x[1:2], x[0:1]], axis=0))

    fin_ref[...] = jnp.zeros_like(fin_ref)
    fin_ref[:, 0:CH] = ordered(pooled)
    fin_ref[:, 1664 : 1664 + CH] = ordered(excite_grad)
    width = squeezed.shape[1]
    fin_ref[:, 3328 : 3328 + width] = ordered(squeezed)
    fin_ref[:, 3712 : 3712 + width] = ordered(squeeze_grad)


def gate_stage(sc, mine, other, w_squeeze, w_excite):
    return pl.pallas_call(
        gate_body,
        out_shape=(
            jax.ShapeDtypeStruct((3, 8, CG), F32),
            jax.ShapeDtypeStruct((2, 4096), F32),
        ),
        in_specs=[SMEM] + [VMEM] * 4,
        out_specs=(VMEM, VMEM),
        scratch_shapes=[pltpu.VMEM((8, CH), F32)],
        compiler_params=params(),
        name="gate_stage",
    )(sc, mine, other, w_squeeze, w_excite)


def outer_dot(a, b):
    ah, am, al = thirds(a)
    bh, bm, bl = thirds(b)
    left = jnp.concatenate([ah, ah, ah, am, am, al], axis=0).astype(BF16)
    right = jnp.concatenate([bh, bm, bl, bh, bm, bh], axis=0).astype(BF16)
    return lax.dot_general(left, right, (((0,), (0,)), ((), ())), preferred_element_type=F32)


def outer_body(width, fin_ref, sq_ref, ex_ref):
    pooled = fin_ref[:, 0:CH]
    excite_grad = fin_ref[:, 1664 : 1664 + CH]
    squeezed = fin_ref[:, 3328 : 3328 + width]
    squeeze_grad = fin_ref[:, 3712 : 3712 + width]
    sq_ref[...] = outer_dot(pooled, squeeze_grad)
    ex_ref[...] = outer_dot(squeezed, excite_grad)


def outer_stage(fin, width):
    return pl.pallas_call(
        functools.partial(outer_body, width),
        out_shape=(
            jax.ShapeDtypeStruct((CH, width), F32),
            jax.ShapeDtypeStruct((width, CH), F32),
        ),
        in_specs=[VMEM],
        out_specs=(VMEM, VMEM),
        compiler_params=params(),
        name="outer_stage",
    )(fin)


def output_body(hid_ref, x3_ref, gate_ref, own_ref, other_ref, wide):
    for g in range(3):
        gate = gate_ref[g]
        by_slide = jnp.concatenate(
            [jnp.broadcast_to(gate[s : s + 1], (16, CG)) for s in range(2)], axis=0
        )
        for i in range(8):
            hidden = hid_ref[g, 32 * i : 32 * i + 32, :]
            active = (hidden * jax.nn.sigmoid(hidden)).astype(BF16).astype(F32)
            value = x3_ref[g, 1, 1 + i].astype(F32) + active * by_slide
            for t in range(4):
                wide[t, 8 * i : 8 * i + 8, CG * g : CG * g + CG] = value[8 * t : 8 * t + 8]
    for t in range(4):
        (own_ref if t < 2 else other_ref)[t % 2] = wide[t].astype(BF16)


def output_stage(hidden, x3, gate):
    shape = jax.ShapeDtypeStruct((2, 64, HALF), BF16)
    return pl.pallas_call(
        output_body,
        out_shape=(shape, shape),
        in_specs=[VMEM] * 3,
        out_specs=(VMEM, VMEM),
        scratch_shapes=[pltpu.VMEM((4, 64, HALF), F32)],
        compiler_params=params(),
        name="output_stage",
    )(hidden, x3, gate)


def backward_body(sizes, sc, hid_ref, x3_ref, cot_ref, w_ref, gate_ref, keep_ref, send_ref, inner_ref, rim_ref,
                  o0, o1, o2, flat, pads, cols):
    g = pl.program_id(0)

    @pl.when(g == 0)
    def _():
        for ref in (o0, o1, o2):
            ref[0:8, :] = jnp.zeros((8, 128), F32)
            ref[TAPROWS:, :] = jnp.zeros((OROWS - TAPROWS, 128), F32)
        pads[...] = jnp.zeros_like(pads)

    hidden = hid_ref[0]
    gate = gate_ref[0]

    def spread(row):
        pair = [jnp.broadcast_to(gate[row + s : row + s + 1], (16, CG)) for s in range(2)]
        both = jnp.concatenate(pair, axis=0)
        return jnp.broadcast_to(both[None], (8, 32, CG)).reshape(256, CG)

    sig = jax.nn.sigmoid(hidden)
    slope = sig * (1.0 + hidden * (1.0 - sig))
    grad = ((cot_ref[0].astype(F32) * spread(0) + spread(2)) * slope).astype(BF16)
    off = jnp.where(sc[0] == 0, 0, 8) + g * (9 * CG)
    zeros = jnp.zeros((CG, 120), F32)
    for dx in range(3):
        for dy in range(3):
            tap = 3 * dy + dx
            x = x3_ref[0, dx, dy : dy + 8].reshape(256, CG)
            res = lax.dot_general(x, grad, (((0,), (0,)), ((), ())), preferred_element_type=F32)
            here = pl.ds(pl.multiple_of(off + CG * tap, 8), CG)
            o0[here, :] = res[:, :128]
            o1[here, :] = res[:, 128:256]
            o2[here, :] = jnp.concatenate([res[:, 256:], zeros], axis=1)
    for dx in range(3):
        cols[...] = jnp.zeros_like(cols)
        for dy in range(3):
            d = lax.dot_general(grad, w_ref[0, 3 * dy + dx], (((1,), (1,)), ((), ())), preferred_element_type=F32)
            cols[dy : dy + 8] += d.reshape(8, 32, CG)
        for value in range(3):
            @pl.when(g == value)
            def _():
                lanes = slice(CG * value, CG * value + CG)
                pads[:, :, dx : dx + 8, lanes] += cols[...].reshape(10, 4, 8, CG)

    @pl.when(g == 2)
    def _():
        for t in range(4):
            for i in range(8):
                inner_ref[t, 8 * i : 8 * i + 8, :] = pads[1 + i, t, 1:9, :]
            left = jnp.concatenate([pads[1 + i, t, 0:1, :] for i in range(8)], axis=0)
            right = jnp.concatenate([pads[1 + i, t, 9:10, :] for i in range(8)], axis=0)
            corners = [pads[0, t, 0:1, :], pads[0, t, 9:10, :], pads[9, t, 0:1, :], pads[9, t, 9:10, :]]
            parts = [pads[0, t, 1:9, :], left, right, pads[9, t, 1:9, :], *corners, jnp.zeros((4, HALF), F32)]
            rim_ref[t] = jnp.concatenate(parts, axis=0).astype(BF16)
        flat[: sizes.top, :] = jnp.zeros((sizes.top, 128), F32)
        base = jnp.where(sc[0] == 0, sizes.top, sizes.top - sizes.bound)

        @pl.loop(0, NCH)
        def _(ch):
            start = base + ch * (33 * PCH)
            carry = None
            for k in range(16):
                where = pl.ds(ch * (16 * PCH) + k, PCH, stride=16)
                x = jnp.concatenate([ref[where, :] for ref in (o0, o1, o2)], axis=1)
                if k:
                    x = pltpu.roll(x, 8 * k, axis=1)
                first = x[:, :128]
                if carry is not None:
                    first = first + carry
                flat[pl.ds(start + 2 * k, PCH, stride=33), :] = first
                flat[pl.ds(start + 2 * k + 1, PCH, stride=33), :] = x[:, 128:256]
                carry = x[:, 256:]
            flat[pl.ds(start + 32, PCH, stride=33), :] = carry

        even = sc[2] == 0
        quarter = sizes.quarter
        rest = sizes.piece - quarter
        for dl in range(sizes.dl_num):
            for q in range(2):
                start = sizes.top + sizes.rows * dl + q * quarter
                v0 = flat[start : start + quarter, :]
                v1 = flat[start + sizes.second : start + sizes.second + quarter, :]
                rel = jnp.bitwise_xor(sc[1], dl)
                part = jnp.bitwise_xor(sc[3], q)
                keep_ref[rel, part, 0:quarter] = jnp.where(even, v0, v1).astype(BF16)
                send_ref[rel, part, 0:quarter] = jnp.where(even, v1, v0).astype(BF16)
                if dl == sizes.dl_num - 1 and q == 1:
                    ext = jnp.concatenate([flat[: sizes.top, :], jnp.zeros((rest - sizes.top, 128), F32)], axis=0) \
                        if rest > sizes.top else flat[: sizes.top, :]
                    keep_ref[rel, part, quarter:] = jnp.where(even, 0.0, ext).astype(BF16)
                    send_ref[rel, part, quarter:] = jnp.where(even, ext, 0.0).astype(BF16)
                else:
                    keep_ref[rel, part, quarter:] = jnp.zeros((rest, 128), BF16)
                    send_ref[rel, part, quarter:] = jnp.zeros((rest, 128), BF16)


def backward(sizes, sc, hidden, x3, cot, w, gate):
    pieces = jax.ShapeDtypeStruct((sizes.dl_num, 2, sizes.piece, 128), BF16)
    return pl.pallas_call(
        functools.partial(backward_body, sizes),
        grid=(3,),
        out_shape=(
            pieces,
            pieces,
            jax.ShapeDtypeStruct((4, 64, HALF), F32),
            jax.ShapeDtypeStruct((4, 40, HALF), BF16),
        ),
        in_specs=[
            SMEM,
            pl.BlockSpec((1, 256, CG), lambda g: (g, 0, 0)),
            pl.BlockSpec((1, 3, 10, 32, CG), lambda g: (g, 0, 0, 0, 0)),
            pl.BlockSpec((1, 256, CG), lambda g: (g, 0, 0)),
            pl.BlockSpec((1, 9, CG, CG), lambda g: (g, 0, 0, 0)),
            pl.BlockSpec((1, 8, CG), lambda g: (g, 0, 0)),
        ],
        out_specs=(VMEM, VMEM, VMEM, VMEM),
        scratch_shapes=[
            pltpu.VMEM((OROWS, 128), F32),
            pltpu.VMEM((OROWS, 128), F32),
            pltpu.VMEM((OROWS, 128), F32),
            pltpu.VMEM((sizes.flat, 128), F32),
            pltpu.VMEM((10, 4, 16, HALF), F32),
            pltpu.VMEM((10, 32, CG), F32),
        ],
        compiler_params=params(),
        name="backward_conv",
    )(sc, hidden, x3, cot, w, gate)


def rims_body(sc, ids, own_ref, other_ref, inner_ref, r0, r1, r2, r3, out0_ref, out1_ref, edges, corners):
    edges[...] = jnp.zeros_like(edges)
    corners[...] = jnp.zeros_like(corners)
    for rel, ref in enumerate((r0, r1, r2, r3)):
        dev = jnp.bitwise_xor(sc[5], rel)
        for slide in range(2):
            for slot in range(2):
                t = 2 * slide + slot
                rim = ref[t].astype(F32)
                for mine in range(2):
                    own = 2 * sc[5] + mine
                    n = 2 * slide + mine

                    def hit(offset):
                        return jnp.where(ids[dev, t, offset] == own, 1.0, 0.0)

                    for member, offset in enumerate((1, 3, 4, 6)):
                        edges[n, member] += hit(offset) * rim[8 * member : 8 * member + 8]
                    for member, offset in enumerate((0, 2, 5, 7)):
                        row = 32 + member
                        corners[n, member : member + 1] += hit(offset) * rim[row : row + 1]
    for n in range(4):
        cot = (own_ref if n < 2 else other_ref)[n % 2].astype(F32)
        inner_ref_n = inner_ref[n] + cot
        last_col = edges[n, 1]
        first_col = edges[n, 2]
        rows = []
        for i in range(8):
            row = inner_ref_n[8 * i : 8 * i + 8]
            lo = first_col[i : i + 1]
            hi = last_col[i : i + 1]
            if i == 0:
                row = row + edges[n, 3]
                hi = hi + corners[n, 2:3]
                lo = lo + corners[n, 3:4]
            if i == 7:
                row = row + edges[n, 0]
                hi = hi + corners[n, 0:1]
                lo = lo + corners[n, 1:2]
            pos = lax.broadcasted_iota(jnp.int32, (8, HALF), 0)
            row = row + jnp.where(pos == 0, lo, 0.0) + jnp.where(pos == 7, hi, 0.0)
            rows.append(row)
        (out0_ref if n < 2 else out1_ref)[n % 2] = jnp.concatenate(rows, axis=0).astype(BF16)


def add_rims(sc, ids, own, other, inner, rims):
    shape = jax.ShapeDtypeStruct((2, 64, HALF), BF16)
    return pl.pallas_call(
        rims_body,
        out_shape=(shape, shape),
        in_specs=[SMEM, SMEM] + [VMEM] * 7,
        out_specs=(VMEM, VMEM),
        scratch_shapes=[
            pltpu.VMEM((4, 4, 8, HALF), F32),
            pltpu.VMEM((4, 8, HALF), F32),
        ],
        compiler_params=params(),
        name="add_rims",
    )(sc, ids, own, other, inner, *rims)


def rows_body(sizes, sc, p0, p1, p2, p3, out_ref, land):
    for rel, ref in enumerate((p0, p1, p2, p3)):
        c = jnp.bitwise_xor(sc[2], rel & 1)
        q = jnp.bitwise_xor(sc[3], rel >> 1)
        land[c, q] = ref[...]
    for c in range(2):
        for q in range(2):
            start = c * sizes.second + q * sizes.quarter
            out_ref[start : start + sizes.quarter, :] = land[c, q].astype(F32)


def place_rows(sizes, sc, parts):
    return pl.pallas_call(
        functools.partial(rows_body, sizes),
        out_shape=jax.ShapeDtypeStruct((sizes.rows, 128), F32),
        in_specs=[SMEM] + [VMEM] * 4,
        out_specs=VMEM,
        scratch_shapes=[pltpu.VMEM((2, 2, sizes.quarter, 128), BF16)],
        compiler_params=params(),
        name="place_rows",
    )(sc, *parts)


def tile_ring(value):
    near = swap(value, "t1")
    far = swap(value, "t0")
    return value, near, far, swap(far, "t1")


def reduce_chunk(value, axes, order):
    current = value.astype(F32)
    names = list(axes)
    for name in order:
        pos = names.index(name)
        send = lax.index_in_dim(current, 1, pos, keepdims=False).astype(BF16)
        stay = lax.index_in_dim(current, 0, pos, keepdims=False)
        current = stay + swap(send, name).astype(F32)
        names.pop(pos)
    return current


def shards(dbits, features, cotangent, conv_weight, squeeze_weight, excite_weight, live_count, neighbours):
    lows = tuple(f"d{i}" for i in range(1, dbits))
    dl_num = 2 ** (dbits - 1)
    sizes = Sizes(conv_weight.shape[0], dl_num)
    dh = lax.axis_index("d0")
    dl = lax.axis_index(lows)
    y = lax.axis_index("t0")
    c = lax.axis_index("t1")
    count = live_count[0, 0]
    sc = jnp.stack([dh, dl, c, y, count, 2 * y + c, count, count]).astype(jnp.int32)

    feat_own, feat_send = split_halves(sc, features.reshape(128, CH))
    feat_other = swap(feat_send, "d0")
    half0 = conv_weight[: sizes.half]
    half1 = conv_weight[sizes.second :]
    bnd = swap(conv_weight[sizes.rows - sizes.top :], "d0")
    if len(lows) == 2:
        mine = jnp.where(c == 0, half0, half1)
        a1 = swap(mine, "d1")
        a2 = swap(mine, "d2")
        b12 = swap(a1[: sizes.quarter], "d2")
        b21 = swap(a2[sizes.quarter :], "d1")
        e1, e2 = swap(a1, "t1"), swap(a2, "t1")
        e12, e21 = swap(b12, "t1"), swap(b21, "t1")
        arrays = [half0, half1, a1, a2, b12, b21, e1, e2, e12, e21]
        plan = [(0, 0), (0, 1), (2, (None, 0)), (1, (None, 0)), (3, (0, 0)), (3, (1, 0)),
                (2, (None, 1)), (1, (None, 1)), (3, (0, 1)), (3, (1, 1))]
        bit1, bit2 = lax.axis_index("d1"), lax.axis_index("d2")
        bnd = jnp.where(bit2 == 1, bnd, swap(bnd, "d2"))
        bnd = jnp.where(bit1 == 1, bnd, swap(bnd, "d1"))
    else:
        arrays = [lax.all_gather(half0, lows), lax.all_gather(half1, lows)]
        plan = [(None, 0), (None, 1)]
        bnd = lax.all_gather(bnd, lows)[-1]

    ids_own = neighbours[0]
    ids4 = jnp.concatenate([ids_own, swap(ids_own, "d0")], axis=0)
    ids_all = lax.all_gather(ids4, ("t0", "t1"))
    cot_own, cot_send = split_halves(sc, cotangent.reshape(128, CH))
    cot_other = swap(cot_send, "d0")
    strips = tile_ring(make_strips(feat_own, feat_other))
    x3 = pad_tiles(sc, ids4, feat_own, feat_other, strips)
    cot = regroup(cot_own, cot_other)
    w = unpack_weight(sizes, sc, plan, arrays, bnd)
    hidden, sums = forward(sc, x3, cot, w)
    sums = sums + swap(sums, "t1")
    sums = sums + swap(sums, "t0")
    gate, fin = gate_stage(sc, sums, swap(sums, "d0"), squeeze_weight, excite_weight)

    keep, send, inner, rims = backward(sizes, sc, hidden, x3, cot, w, gate)

    total = keep.astype(F32) + swap(send, "t1").astype(F32)
    axes = lows + ("t0",)
    total = total.reshape((2,) * len(axes) + (sizes.piece, 128))
    chunk = sizes.piece // 3
    done = []
    for part in range(3):
        turn = (len(axes) - 1 + part) % len(axes)
        order = axes[turn:] + axes[:turn]
        done.append(reduce_chunk(total[..., part * chunk : (part + 1) * chunk, :], axes, order))
    summed = jnp.concatenate(done, axis=0)
    ext = summed[sizes.quarter : sizes.quarter + sizes.top].astype(BF16)
    ext = jnp.where(dh == 0, swap(ext, "d0").astype(F32), 0.0)
    body = summed[: sizes.quarter]
    body = body.at[sizes.quarter - sizes.top :].add(ext).astype(BF16)
    grad_conv = place_rows(sizes, sc, tile_ring(body))

    back_own, back_send = add_rims(sc, ids_all, cot_own, cot_other, inner, tile_ring(rims))
    grad_in = join_halves(sc, back_own, swap(back_send, "d0"))

    out_own, out_send = output_stage(hidden, x3, gate)
    output = join_halves(sc, out_own, swap(out_send, "d0"))

    for name in reversed(lows):
        got = swap(fin, name)
        first = lax.axis_index(name) == 0
        fin = jnp.concatenate([jnp.where(first, fin, got), jnp.where(first, got, fin)], axis=0)
    grad_squeeze, grad_excite = outer_stage(fin, squeeze_weight.shape[1])
    shape = features.shape
    return (output.reshape(shape), grad_in.reshape(shape), grad_conv, grad_squeeze, grad_excite)


def solution(mesh):
    dbits = mesh.shape["dp"].bit_length() - 1
    dnames = tuple(f"d{i}" for i in range(dbits))
    tnames = ("t0", "t1")
    fine = Mesh(mesh.devices.reshape((2,) * (dbits + 2)), dnames + tnames)
    return jax.shard_map(
        functools.partial(shards, dbits),
        mesh=fine,
        in_specs=(
            P(dnames, tnames, None, None, None),
            P(dnames, tnames, None, None, None),
            P(dnames, None),
            P(),
            P(),
            P(dnames, tnames),
            P(dnames, tnames, None),
        ),
        out_specs=(
            P(dnames, tnames, None, None, None),
            P(dnames, tnames, None, None, None),
            P(dnames, None),
            P(),
            P(),
        ),
        check_vma=False,
    )
```

```python
import functools

import jax
import jax.numpy as jnp
from jax import lax
from jax.experimental import pallas as pl
from jax.experimental.pallas import tpu as pltpu
from jax.sharding import Mesh, PartitionSpec as P

CG = 264
HALF = 3 * CG
TAPROWS = 27 * CG
LEAD = 33 * (TAPROWS // 16)
CH = 2 * HALF
F32 = jnp.float32
BF16 = jnp.bfloat16
SWAP = [(0, 1), (1, 0)]
PCH = 64
NCH = 7
OROWS = 16 * PCH * NCH + 8
VMEM = pl.BlockSpec(memory_space=pltpu.VMEM)
SMEM = pl.BlockSpec(memory_space=pltpu.SMEM)
HBM = pl.BlockSpec(memory_space=pltpu.HBM)


def params(mebibytes):
    return pltpu.CompilerParams(vmem_limit_bytes=mebibytes * 1024 * 1024)


def cost(microseconds):
    return pl.CostEstimate(flops=0, bytes_accessed=int(microseconds * 0.05 * 3.6e6), transcendentals=0)


def swap(value, axis):
    return lax.ppermute(value, axis, SWAP)


class Sizes:
    def __init__(self, rows, dl_num):
        self.rows = rows
        self.dl_num = dl_num
        self.bound = rows * dl_num - LEAD
        self.top = -(-self.bound // 16) * 16
        self.half = -(-rows // 64) * 32
        self.second = rows - self.half
        self.quarter = self.half // 2
        self.flat = self.top + 33 * PCH * NCH + 8


def split_body(sc, x_ref, mine_ref, send_ref):
    low = sc[0] == 0
    for slot in range(2):
        x = x_ref[64 * slot : 64 * slot + 64, :]
        x = jnp.where(slot < sc[4], x, jnp.zeros_like(x))
        first, second = x[:, :HALF], x[:, HALF:]
        mine_ref[slot] = jnp.where(low, first, second)
        send_ref[slot] = jnp.where(low, second, first)


def split_halves(sc, x):
    shape = jax.ShapeDtypeStruct((2, 64, HALF), BF16)
    return pl.pallas_call(
        split_body,
        out_shape=(shape, shape),
        in_specs=[SMEM, VMEM],
        out_specs=(VMEM, VMEM),
        compiler_params=params(10),
        cost_estimate=cost(2),
        name="split_halves",
    )(sc, x)


def join_body(sc, a_ref, b_ref, out_ref, wide):
    low = sc[0] == 0
    for slot in range(2):
        a = a_ref[slot].astype(F32)
        b = b_ref[slot].astype(F32)
        live = slot < sc[4]
        first = jnp.where(low, a, b)
        second = jnp.where(low, b, a)
        wide[:, :HALF] = jnp.where(live, first, 0.0)
        wide[:, HALF:] = jnp.where(live, second, 0.0)
        out_ref[64 * slot : 64 * slot + 64, :] = wide[...].astype(BF16)


def join_halves(sc, a, b):
    return pl.pallas_call(
        join_body,
        out_shape=jax.ShapeDtypeStruct((128, CH), BF16),
        in_specs=[SMEM, VMEM, VMEM],
        out_specs=VMEM,
        scratch_shapes=[pltpu.VMEM((64, CH), F32)],
        compiler_params=params(10),
        cost_estimate=cost(2),
        name="join_halves",
    )(sc, a, b)


def strips_body(own_ref, other_ref, out_ref):
    for t in range(4):
        ref = own_ref if t < 2 else other_ref
        x = ref[t % 2].astype(F32)
        cube = x.reshape(8, 8, HALF)
        out = jnp.concatenate([x[:8], x[56:], cube[:, 0, :], cube[:, 7, :]], axis=0)
        out_ref[t] = out.astype(BF16)


def make_strips(own, other):
    return pl.pallas_call(
        strips_body,
        out_shape=jax.ShapeDtypeStruct((4, 32, HALF), BF16),
        in_specs=[VMEM, VMEM],
        out_specs=VMEM,
        compiler_params=params(10),
        cost_estimate=cost(1.9),
        name="make_strips",
    )(own, other)


def pad_body(sc, ids, own_ref, other_ref, s0, s1, s2, s3, x3_ref, strips, pad):
    for rel, ref in enumerate((s0, s1, s2, s3)):
        strips[rel] = ref[...]
    for t in range(4):
        ref = own_ref if t < 2 else other_ref
        x = ref[t % 2].astype(F32)
        for i in range(8):
            pad[1 + i, t, 1:9, :] = x[8 * i : 8 * i + 8]

        def piece(offset, member):
            n = ids[t, offset]
            safe = jnp.maximum(n, 0)
            rel = jnp.bitwise_xor(lax.shift_right_logical(safe, 1), sc[5])
            other = 2 * (t // 2) + jnp.bitwise_and(safe, 1)
            got = strips[rel, other].astype(F32)[8 * member : 8 * member + 8]
            return jnp.where(n >= 0, got, 0.0)

        pad[0, t, 0:1, :] = piece(0, 1)[7:8]
        pad[0, t, 1:9, :] = piece(1, 1)
        pad[0, t, 9:10, :] = piece(2, 1)[0:1]
        left = piece(3, 3)
        right = piece(4, 2)
        for i in range(8):
            pad[1 + i, t, 0:1, :] = left[i : i + 1]
            pad[1 + i, t, 9:10, :] = right[i : i + 1]
        pad[9, t, 0:1, :] = piece(5, 0)[7:8]
        pad[9, t, 1:9, :] = piece(6, 0)
        pad[9, t, 9:10, :] = piece(7, 0)[0:1]
    for i in range(10):
        for dx in range(3):
            row = pad[i, :, dx : dx + 8, :].reshape(32, HALF)
            for g in range(3):
                x3_ref[g, dx, i] = row[:, CG * g : CG * g + CG].astype(BF16)


def pad_tiles(sc, ids, own, other, strips):
    return pl.pallas_call(
        pad_body,
        out_shape=jax.ShapeDtypeStruct((3, 3, 10, 32, CG), BF16),
        in_specs=[SMEM, SMEM] + [VMEM] * 6,
        out_specs=VMEM,
        scratch_shapes=[
            pltpu.VMEM((4, 4, 32, HALF), BF16),
            pltpu.VMEM((10, 4, 16, HALF), F32),
        ],
        compiler_params=params(20),
        cost_estimate=cost(3.8),
        name="pad_tiles",
    )(sc, ids, own, other, *strips)


def weight_body(sizes, plan, sc, *refs):
    count = len(plan)
    srcs = refs[:count]
    x3_hbm, w_ref, hid_ref, sums_ref, land, tails, flat, o0, o1, o2, built, x3, sems, more = refs[count:]
    load = pltpu.make_async_copy(x3_hbm, x3, more.at[3])
    copies = []
    for pos, (kind, rel, half, quarter) in enumerate(plan):
        src = srcs[pos]
        pairs = []
        if kind == "all":
            pairs.append((src, land.at[:, half]))
        elif kind == "tail":
            pairs.append((src, tails.at[rel]))
        else:
            dl = jnp.bitwise_xor(sc[1], rel)
            if kind == "own":
                pairs.append((src, land.at[dl, half]))
            elif kind == "half":
                pairs.append((src, land.at[dl, jnp.bitwise_xor(sc[2], half)]))
            else:
                start = pl.multiple_of(jnp.bitwise_xor(sc[3], quarter) * sizes.quarter, 16)
                slot = land.at[dl, jnp.bitwise_xor(sc[2], half), pl.ds(start, sizes.quarter)]
                pairs.append((src.at[pl.ds(0, sizes.quarter)], slot))
                if rel == 2:
                    pairs.append((src.at[pl.ds(sizes.quarter, sizes.top)], tails.at[2 * quarter + half]))
        for src, dst in pairs:
            copies.append(pltpu.make_async_copy(src, dst, sems.at[len(copies)]))
            copies[-1].start()
    load.start()
    for copy in copies:
        copy.wait()
    last = 0 if plan[0][0] == "all" else jnp.bitwise_xor(sc[1], sc[5])
    flat[: sizes.top, :] = tails[last].astype(F32)
    for dl in range(sizes.dl_num):
        start = sizes.top + sizes.rows * dl
        flat[start : start + sizes.half, :] = land[dl, 0].astype(F32)
        start += sizes.second
        flat[start : start + sizes.half, :] = land[dl, 1].astype(F32)
    base = jnp.where(sc[0] == 0, sizes.top, sizes.top - sizes.bound)

    @pl.loop(0, NCH)
    def _(ch):
        start = base + ch * (33 * PCH)
        for k in range(16):
            rows = [flat[pl.ds(start + 2 * k + j, PCH, stride=33), :] for j in range(3)]
            x = jnp.concatenate(rows, axis=1)
            if k:
                x = pltpu.roll(x, 384 - 8 * k, axis=1)
            for col, ref in enumerate((o0, o1, o2)):
                ref[pl.ds(ch * (16 * PCH) + k, PCH, stride=16), :] = x[:, 128 * col : 128 * col + 128]

    off = jnp.where(sc[0] == 0, 0, 8)
    stores = []
    for g in range(3):
        for tap in range(9):
            here = pl.ds(pl.multiple_of(off + CG * (9 * g + tap), 8), CG)
            built[g, tap, :, :128] = o0[here, :].astype(BF16)
            built[g, tap, :, 128:256] = o1[here, :].astype(BF16)
            built[g, tap, :, 256:] = o2[here, :8].astype(BF16)
        stores.append(pltpu.make_async_copy(built.at[g], w_ref.at[g], more.at[g]))
        stores[g].start()
        if g == 0:
            load.wait()
        forward_group(sc, g, x3, built, hid_ref, sums_ref)
    for copy in stores:
        copy.wait()


def forward_group(sc, g, x3, w, hid_ref, sums_ref):
    acc = jnp.zeros((256, CG), F32)
    for dx in range(3):
        for dy in range(3):
            x = x3[g, dx, dy : dy + 8].reshape(256, CG)
            acc += jnp.dot(x, w[g, 3 * dy + dx], preferred_element_type=F32)
    hid_ref[g] = acc
    active = (acc * jax.nn.sigmoid(acc)).astype(BF16).astype(F32)
    sums_ref[g] = jnp.full((8, CG), sc[4].astype(F32), F32)
    slide_sums(active, sums_ref, g, 0)


def slide_sums(value, sums_ref, g, row):
    value = value.reshape(8, 4, 8, CG)
    for slide in range(2):
        part = value[:, 2 * slide] + value[:, 2 * slide + 1]
        sums_ref[g, row + slide : row + slide + 1, :] = jnp.sum(jnp.sum(part, axis=0), axis=0, keepdims=True)


def weight_forward(sizes, sc, plan, arrays, x3):
    return pl.pallas_call(
        functools.partial(weight_body, sizes, plan),
        out_shape=(
            jax.ShapeDtypeStruct((3, 9, CG, CG), BF16),
            jax.ShapeDtypeStruct((3, 256, CG), F32),
            jax.ShapeDtypeStruct((3, 8, CG), F32),
        ),
        in_specs=[SMEM] + [HBM] * (len(plan) + 1),
        out_specs=(HBM, VMEM, VMEM),
        scratch_shapes=[
            pltpu.VMEM((sizes.dl_num, 2, sizes.half, 128), BF16),
            pltpu.VMEM((4, sizes.top, 128), BF16),
            pltpu.VMEM((sizes.flat, 128), F32),
            pltpu.VMEM((OROWS, 128), F32),
            pltpu.VMEM((OROWS, 128), F32),
            pltpu.VMEM((OROWS, 128), F32),
            pltpu.VMEM((3, 9, CG, CG), BF16),
            pltpu.VMEM((3, 3, 10, 32, CG), BF16),
            pltpu.SemaphoreType.DMA((len(plan) + 4,)),
            pltpu.SemaphoreType.DMA((4,)),
        ],
        compiler_params=params(48),
        cost_estimate=cost(18),
        name="weight_forward",
    )(sc, *arrays, x3)


def regroup_body(own_ref, other_ref, hid_ref, half_ref, out_ref, sums_ref, cot):
    x = [(own_ref if t < 2 else other_ref)[t % 2].astype(F32) for t in range(4)]
    for i in range(8):
        row = jnp.concatenate([x[t][8 * i : 8 * i + 8] for t in range(4)], axis=0)
        for g in range(3):
            part = row[:, CG * g : CG * g + CG]
            out_ref[g, 32 * i : 32 * i + 32, :] = part.astype(BF16)
            cot[g, 32 * i : 32 * i + 32, :] = part
    for g in range(3):
        hidden = hid_ref[g]
        active = (hidden * jax.nn.sigmoid(hidden)).astype(BF16).astype(F32)
        sums_ref[g] = half_ref[g]
        slide_sums(active * cot[g], sums_ref, g, 2)


def regroup(own, other, hidden, sums):
    return pl.pallas_call(
        regroup_body,
        out_shape=(
            jax.ShapeDtypeStruct((3, 256, CG), BF16),
            jax.ShapeDtypeStruct((3, 8, CG), F32),
        ),
        in_specs=[VMEM] * 4,
        out_specs=(VMEM, VMEM),
        scratch_shapes=[pltpu.VMEM((3, 256, CG), F32)],
        compiler_params=params(12),
        cost_estimate=cost(3.3),
        name="regroup",
    )(own, other, hidden, sums)


def thirds(x):
    hi = x.astype(BF16).astype(F32)
    mid = (x - hi).astype(BF16).astype(F32)
    low = (x - hi - mid).astype(BF16).astype(F32)
    return hi, mid, low


def exact_dot(x, w, contract):
    parts = jnp.concatenate([*thirds(x), jnp.zeros((10, x.shape[1]), F32)], axis=0).astype(BF16)
    out = lax.dot_general(parts, w, (((1,), (contract,)), ((), ())), preferred_element_type=F32)
    return out[0:2] + out[2:4] + out[4:6]


def gate_body(sc, mine_ref, mine_far_ref, other_ref, other_far_ref, sq_ref, ex_ref, gate_ref, fin_ref, wide):
    low = sc[0] == 0
    for g in range(3):
        a = mine_ref[g] + mine_far_ref[g]
        b = other_ref[g] + other_far_ref[g]
        if g == 0:
            counts = jnp.concatenate([a[4:5, 0:1], b[4:5, 0:1]], axis=0)
        a = a[0:4]
        b = jnp.concatenate([b[1:2], b[0:1], b[3:4], b[2:3]], axis=0)
        wide[0:4, CG * g : CG * g + CG] = jnp.where(low, a, b)
        wide[0:4, HALF + CG * g : HALF + CG * g + CG] = jnp.where(low, b, a)
    total = counts * 64.0
    pooled = wide[0:2, :] / total
    gate = wide[2:4, :]
    w_squeeze = sq_ref[...]
    w_excite = ex_ref[...]
    pre = exact_dot(pooled, w_squeeze, 0)
    sig = jax.nn.sigmoid(pre)
    squeezed = pre * sig
    excite = jax.nn.sigmoid(exact_dot(squeezed, w_excite, 1))
    excite_grad = gate * excite * (1.0 - excite)
    slope = sig * (1.0 + pre * (1.0 - sig))
    squeeze_grad = exact_dot(excite_grad, w_excite, 0) * slope
    pool = exact_dot(squeeze_grad, w_squeeze, 1) / total
    half_e = jnp.where(low, excite[:, :HALF], excite[:, HALF:])
    half_p = jnp.where(low, pool[:, :HALF], pool[:, HALF:])
    for g in range(3):
        gate_ref[g, 0:2, :] = half_e[:, CG * g : CG * g + CG]
        gate_ref[g, 2:4, :] = half_p[:, CG * g : CG * g + CG]

    def ordered(x):
        return jnp.where(low, x, jnp.concatenate([x[1:2], x[0:1]], axis=0))

    fin_ref[...] = jnp.zeros_like(fin_ref)
    fin_ref[:, 0:CH] = ordered(pooled)
    fin_ref[:, 1664 : 1664 + CH] = ordered(excite_grad)
    width = squeezed.shape[1]
    fin_ref[:, 3328 : 3328 + width] = ordered(squeezed)
    fin_ref[:, 3712 : 3712 + width] = ordered(squeeze_grad)


def gate_stage(sc, sums, w_squeeze, w_excite):
    return pl.pallas_call(
        gate_body,
        out_shape=(
            jax.ShapeDtypeStruct((3, 8, CG), F32),
            jax.ShapeDtypeStruct((2, 4096), F32),
        ),
        in_specs=[SMEM] + [VMEM] * 6,
        out_specs=(VMEM, VMEM),
        scratch_shapes=[pltpu.VMEM((8, CH), F32)],
        compiler_params=params(16),
        cost_estimate=cost(3.9),
        name="gate_stage",
    )(sc, *sums, w_squeeze, w_excite)


def outer_dot(a, b):
    ah, am, al = thirds(a)
    bh, bm, bl = thirds(b)
    left = jnp.concatenate([ah, ah, ah, am, am, al], axis=0).astype(BF16)
    right = jnp.concatenate([bh, bm, bl, bh, bm, bh], axis=0).astype(BF16)
    return lax.dot_general(left, right, (((0,), (0,)), ((), ())), preferred_element_type=F32)


def outer_body(width, fin_ref, sq_ref, ex_ref):
    pooled = fin_ref[:, 0:CH]
    excite_grad = fin_ref[:, 1664 : 1664 + CH]
    squeezed = fin_ref[:, 3328 : 3328 + width]
    squeeze_grad = fin_ref[:, 3712 : 3712 + width]
    sq_ref[...] = outer_dot(pooled, squeeze_grad)
    ex_ref[...] = outer_dot(excite_grad, squeezed)


def outer_stage(fin, width):
    return pl.pallas_call(
        functools.partial(outer_body, width),
        out_shape=(
            jax.ShapeDtypeStruct((CH, width), F32),
            jax.ShapeDtypeStruct((CH, width), F32),
        ),
        in_specs=[VMEM],
        out_specs=(VMEM, VMEM),
        compiler_params=params(20),
        cost_estimate=cost(3.7),
        name="outer_stage",
    )(fin)


def output_body(hid_ref, x3_ref, gate_ref, own_ref, other_ref, wide):
    for g in range(3):
        gate = gate_ref[g]
        by_slide = jnp.concatenate(
            [jnp.broadcast_to(gate[s : s + 1], (16, CG)) for s in range(2)], axis=0
        )
        for i in range(8):
            hidden = hid_ref[g, 32 * i : 32 * i + 32, :]
            active = (hidden * jax.nn.sigmoid(hidden)).astype(BF16).astype(F32)
            value = x3_ref[g, 1, 1 + i].astype(F32) + active * by_slide
            for t in range(4):
                wide[t, 8 * i : 8 * i + 8, CG * g : CG * g + CG] = value[8 * t : 8 * t + 8]
    for t in range(4):
        (own_ref if t < 2 else other_ref)[t % 2] = wide[t].astype(BF16)


def output_stage(hidden, x3, gate):
    shape = jax.ShapeDtypeStruct((2, 64, HALF), BF16)
    return pl.pallas_call(
        output_body,
        out_shape=(shape, shape),
        in_specs=[VMEM] * 3,
        out_specs=(VMEM, VMEM),
        scratch_shapes=[pltpu.VMEM((4, 64, HALF), F32)],
        compiler_params=params(16),
        cost_estimate=cost(3.1),
        name="output_stage",
    )(hidden, x3, gate)


def hidden_slope(hid_ref, cot_ref, gate_ref):
    hidden = hid_ref[0]
    gate = gate_ref[0]

    def spread(row):
        pair = [jnp.broadcast_to(gate[row + s : row + s + 1], (16, CG)) for s in range(2)]
        both = jnp.concatenate(pair, axis=0)
        return jnp.broadcast_to(both[None], (8, 32, CG)).reshape(256, CG)

    sig = jax.nn.sigmoid(hidden)
    slope = sig * (1.0 + hidden * (1.0 - sig))
    return ((cot_ref[0].astype(F32) * spread(0) + spread(2)) * slope).astype(BF16)


def weight_grad_body(sizes, sc, grad_ref, x3_ref, keep_ref, send_ref, ext_ref, flat, carry):
    g = pl.program_id(0)

    @pl.when(g == 0)
    def _():
        end = sizes.top + sizes.rows * sizes.dl_num
        flat[: sizes.top, :] = jnp.zeros((sizes.top, 128), F32)
        flat[end - 16 : end, :] = jnp.zeros((16, 128), F32)
        carry[...] = jnp.zeros_like(carry)

    grad = grad_ref[0]
    base = jnp.where(sc[0] == 0, sizes.top, sizes.top - sizes.bound)
    first = jnp.where(sc[0] == 0, 0, 1) + g * (9 * 33)
    row = lax.broadcasted_iota(jnp.int32, (8, 128), 0)
    lane = lax.broadcasted_iota(jnp.int32, (8, 128), 1)
    edge = lane - 8 * row
    zeros = jnp.zeros((CG, 120), F32)

    def taps(odd):
        held = carry[...]
        for tap in range(9):
            dy, dx = divmod(tap, 3)
            x = x3_ref[0, dx, dy : dy + 8].reshape(256, CG)
            res = lax.dot_general(x, grad, (((0,), (0,)), ((), ())), preferred_element_type=F32)
            res = jnp.concatenate([res, zeros], axis=1)
            for i in range(33):
                h = (odd + tap + i) % 2
                place = first + 33 * tap + i
                start = base + 33 * lax.shift_right_logical(place, 1) + 16 * h
                turned = [
                    pltpu.roll(
                        res[8 * i : 8 * i + 8, 128 * col : 128 * col + 128], 64 * h, axis=1, stride=8, stride_axis=0
                    )
                    for col in range(3)
                ]
                own = edge >= 64 * h
                third = jnp.where(own, turned[2], turned[1])
                shifted = pltpu.roll(third, 1, axis=0)
                before = jnp.where(row == 0, held, shifted)
                flat[pl.ds(start, 8, stride=2), :] = jnp.where(own, turned[0], before)
                flat[pl.ds(start + 1, 8, stride=2), :] = jnp.where(own, turned[1], turned[0])
                flat[pl.ds(start + 16, 1), :] = third[7:8]
                held = shifted
        carry[...] = held

    parity = jnp.bitwise_and(first, 1)
    for odd in range(2):
        @pl.when(parity == odd)
        def _():
            taps(odd)

    @pl.when(g == 2)
    def _():
        even = sc[2] == 0
        quarter = sizes.quarter
        ext_ref[...] = flat[: sizes.top, :]
        for dl in range(sizes.dl_num):
            for q in range(2):
                start = sizes.top + sizes.rows * dl + q * quarter
                v0 = flat[start : start + quarter, :]
                v1 = flat[start + sizes.second : start + sizes.second + quarter, :]
                rel = jnp.bitwise_xor(sc[1], dl)
                part = jnp.bitwise_xor(sc[3], q)
                keep_ref[rel, part] = jnp.where(even, v0, v1).astype(BF16)
                send_ref[rel, part] = jnp.where(even, v1, v0).astype(BF16)


def weight_grad(sizes, sc, grad, x3):
    pieces = jax.ShapeDtypeStruct((sizes.dl_num, 2, sizes.quarter, 128), BF16)
    return pl.pallas_call(
        functools.partial(weight_grad_body, sizes),
        grid=(3,),
        out_shape=(
            pieces,
            pieces,
            jax.ShapeDtypeStruct((sizes.top, 128), F32),
        ),
        in_specs=[
            SMEM,
            pl.BlockSpec((1, 256, CG), lambda g: (g, 0, 0)),
            pl.BlockSpec((1, 3, 10, 32, CG), lambda g: (g, 0, 0, 0, 0)),
        ],
        out_specs=(VMEM, VMEM, VMEM),
        scratch_shapes=[
            pltpu.VMEM((sizes.flat, 128), F32),
            pltpu.VMEM((8, 128), F32),
        ],
        compiler_params=params(32),
        cost_estimate=cost(11.9),
        name="weight_grad",
    )(sc, grad, x3)


def input_grad_body(ids, hid_ref, cot_ref, gate_ref, w_ref, inner_ref, rim_ref, grad_ref, pads, part, cols):
    g = pl.program_id(0)

    part[...] = jnp.zeros_like(part)
    grad = hidden_slope(hid_ref, cot_ref, gate_ref)
    grad_ref[0] = grad
    for dx in range(3):
        cols[...] = jnp.zeros_like(cols)
        for dy in range(3):
            d = lax.dot_general(grad, w_ref[0, 3 * dy + dx], (((1,), (1,)), ((), ())), preferred_element_type=F32)
            cols[dy : dy + 8] += d.reshape(8, 32, CG)
        part[:, :, dx : dx + 8, :] += cols[...].reshape(10, 4, 8, CG)
    for value in range(3):
        @pl.when(g == value)
        def _():
            pads[:, :, :, CG * value : CG * value + CG] = part[...]

    @pl.when(g == 2)
    def _():
        for t in range(4):
            for i in range(8):
                inner_ref[t, 8 * i : 8 * i + 8, :] = pads[1 + i, t, 1:9, :]
            left = jnp.concatenate([pads[1 + i, t, 0:1, :] for i in range(8)], axis=0)
            right = jnp.concatenate([pads[1 + i, t, 9:10, :] for i in range(8)], axis=0)
            corners = [pads[0, t, 0:1, :], pads[0, t, 9:10, :], pads[9, t, 0:1, :], pads[9, t, 9:10, :]]
            lane = lax.broadcasted_iota(jnp.int32, (4, HALF), 1)
            listed = jnp.full((4, HALF), -1.0, F32)
            for k in range(8):
                listed = jnp.where(lane == k, ids[t, k].astype(F32), listed)
            parts = [pads[0, t, 1:9, :], left, right, pads[9, t, 1:9, :], *corners, listed]
            rim_ref[t] = jnp.concatenate(parts, axis=0).astype(BF16)


def input_grad(ids, hidden, cot, gate, w):
    return pl.pallas_call(
        input_grad_body,
        grid=(3,),
        out_shape=(
            jax.ShapeDtypeStruct((4, 64, HALF), F32),
            jax.ShapeDtypeStruct((4, 40, HALF), BF16),
            jax.ShapeDtypeStruct((3, 256, CG), BF16),
        ),
        in_specs=[
            SMEM,
            pl.BlockSpec((1, 256, CG), lambda g: (g, 0, 0)),
            pl.BlockSpec((1, 256, CG), lambda g: (g, 0, 0)),
            pl.BlockSpec((1, 8, CG), lambda g: (g, 0, 0)),
            pl.BlockSpec((1, 9, CG, CG), lambda g: (g, 0, 0, 0)),
        ],
        out_specs=(VMEM, VMEM, pl.BlockSpec((1, 256, CG), lambda g: (g, 0, 0))),
        scratch_shapes=[
            pltpu.VMEM((10, 4, 16, HALF), F32),
            pltpu.VMEM((10, 4, 16, CG), F32),
            pltpu.VMEM((10, 32, CG), F32),
        ],
        compiler_params=params(28),
        cost_estimate=cost(9.5),
        name="input_grad",
    )(ids, hidden, cot, gate, w)


def rims_body(sc, own_ref, other_ref, inner_ref, r0, r1, r2, r3, out0_ref, out1_ref, edges, corners):
    edges[...] = jnp.zeros_like(edges)
    corners[...] = jnp.zeros_like(corners)
    for ref in (r0, r1, r2, r3):
        for slide in range(2):
            for slot in range(2):
                t = 2 * slide + slot
                rim = ref[t].astype(F32)
                for mine in range(2):
                    own = (2 * sc[5] + mine).astype(F32)
                    n = 2 * slide + mine

                    def hit(offset):
                        return jnp.where(rim[36:37, offset : offset + 1] == own, 1.0, 0.0)

                    for member, offset in enumerate((1, 3, 4, 6)):
                        edges[n, member] += hit(offset) * rim[8 * member : 8 * member + 8]
                    for member, offset in enumerate((0, 2, 5, 7)):
                        row = 32 + member
                        corners[n, member : member + 1] += hit(offset) * rim[row : row + 1]
    for n in range(4):
        cot = (own_ref if n < 2 else other_ref)[n % 2].astype(F32)
        inner_ref_n = inner_ref[n] + cot
        last_col = edges[n, 1]
        first_col = edges[n, 2]
        rows = []
        for i in range(8):
            row = inner_ref_n[8 * i : 8 * i + 8]
            lo = first_col[i : i + 1]
            hi = last_col[i : i + 1]
            if i == 0:
                row = row + edges[n, 3]
                hi = hi + corners[n, 2:3]
                lo = lo + corners[n, 3:4]
            if i == 7:
                row = row + edges[n, 0]
                hi = hi + corners[n, 0:1]
                lo = lo + corners[n, 1:2]
            pos = lax.broadcasted_iota(jnp.int32, (8, HALF), 0)
            row = row + jnp.where(pos == 0, lo, 0.0) + jnp.where(pos == 7, hi, 0.0)
            rows.append(row)
        (out0_ref if n < 2 else out1_ref)[n % 2] = jnp.concatenate(rows, axis=0).astype(BF16)


def add_rims(sc, own, other, inner, rims):
    shape = jax.ShapeDtypeStruct((2, 64, HALF), BF16)
    return pl.pallas_call(
        rims_body,
        out_shape=(shape, shape),
        in_specs=[SMEM] + [VMEM] * 7,
        out_specs=(VMEM, VMEM),
        scratch_shapes=[
            pltpu.VMEM((4, 4, 8, HALF), F32),
            pltpu.VMEM((4, 8, HALF), F32),
        ],
        compiler_params=params(16),
        cost_estimate=cost(3.4),
        name="add_rims",
    )(sc, own, other, inner, *rims)


def rows_body(sizes, sc, p0, p1, p2, p3, out_ref, land, sems):
    copies = []
    for rel, ref in enumerate((p0, p1, p2, p3)):
        c = jnp.bitwise_xor(sc[2], rel & 1)
        q = jnp.bitwise_xor(sc[3], rel >> 1)
        copies.append(pltpu.make_async_copy(ref, land.at[c, q], sems.at[rel]))
        copies[-1].start()
    for copy in copies:
        copy.wait()
    for c in range(2):
        for q in range(2):
            start = c * sizes.second + q * sizes.quarter
            out_ref[start : start + sizes.quarter, :] = land[c, q].astype(F32)


def place_rows(sizes, sc, parts):
    return pl.pallas_call(
        functools.partial(rows_body, sizes),
        out_shape=jax.ShapeDtypeStruct((sizes.rows, 128), F32),
        in_specs=[SMEM] + [HBM] * 4,
        out_specs=VMEM,
        scratch_shapes=[
            pltpu.VMEM((2, 2, sizes.quarter, 128), BF16),
            pltpu.SemaphoreType.DMA((4,)),
        ],
        compiler_params=params(12),
        cost_estimate=cost(3),
        name="place_rows",
    )(sc, *parts)


def tile_ring(value):
    near = swap(value, "t1")
    far = swap(value, "t0")
    return value, near, far, swap(far, "t1")


def tie(*values):
    return lax.optimization_barrier(values)


def grow(value, name):
    other = swap(value, name)
    first = lax.axis_index(name) == 0
    return jnp.concatenate([jnp.where(first, value, other), jnp.where(first, other, value)], axis=0)


def halve(current, names, name):
    pos = names.index(name)
    send = lax.index_in_dim(current, 1, pos, keepdims=False).astype(BF16)
    stay = lax.index_in_dim(current, 0, pos, keepdims=False)
    return send, stay, [n for n in names if n != name]


def shards(dbits, features, cotangent, conv_weight, squeeze_weight, excite_weight, live_count, neighbours):
    lows = tuple(f"d{i}" for i in range(1, dbits))
    dl_num = 2 ** (dbits - 1)
    sizes = Sizes(conv_weight.shape[0], dl_num)
    dh = lax.axis_index("d0")
    dl = lax.axis_index(lows)
    y = lax.axis_index("t0")
    c = lax.axis_index("t1")
    count = live_count[0, 0]
    sc = jnp.stack([dh, dl, c, y, count, 2 * y + c, count, count]).astype(jnp.int32)

    half0 = conv_weight[: sizes.half]
    half1 = conv_weight[sizes.second :]
    tail = conv_weight[sizes.rows - sizes.top :]
    ids_own = neighbours[0]
    if len(lows) == 2:
        mine = jnp.where(c == 0, half0, half1)
        part = jnp.where(y == 0, mine[: sizes.quarter], mine[sizes.quarter :])
        mine, part, features = tie(mine, part, features)
        a2 = swap(mine, "d2")
        q1 = swap(part, "d1")
        bnd = lax.ppermute(tail, ("d0",) + lows + ("t0", "t1"), [(12 + t, 16 + 5 * t) for t in range(4)])
        feat_own, feat_send = split_halves(sc, features.reshape(128, CH))
        feat_other = swap(feat_send, "d0")
        ids4 = jnp.concatenate([ids_own, swap(ids_own, "d0")], axis=0)
        s0 = make_strips(feat_own, feat_other)
        q1, feat_own = tie(q1, feat_own)
        q3 = swap(q1, "d2")
        q1 = jnp.concatenate([q1, bnd], axis=0)
        y1 = swap(q1, "t0")
        s0, y1, q3, ids4, cotangent = tie(s0, y1, q3, ids4, cotangent)
        cot_own, cot_send = split_halves(sc, cotangent.reshape(128, CH))
        s1, s2 = swap(s0, "t1"), swap(s0, "t0")
        s1, s2, q3, y1, cot_send = tie(s1, s2, q3, y1, cot_send)
        y3 = swap(q3, "t0")
        cot_other = swap(cot_send, "d0")
        strips = [s0, s1, s2, swap(s2, "t1")]
        near = [swap(p, "t1") for p in (a2, q1, q3, y1)]
        x3 = pad_tiles(sc, ids4, feat_own, feat_other, strips)
        y3, x3 = tie(y3, x3)
        arrays = [bnd, half0, half1, a2, q1, q3, y1, y3, *near, swap(y3, "t1")]
        plan = [("tail", 0, 0, 0), ("own", 0, 0, 0), ("own", 0, 1, 0)]
        for half in range(2):
            plan += [("half", 1, half, 0), ("quarter", 2, half, 0), ("quarter", 3, half, 0),
                     ("quarter", 2, half, 1), ("quarter", 3, half, 1)]
    else:
        feat_own, feat_send = split_halves(sc, features.reshape(128, CH))
        feat_other = swap(feat_send, "d0")
        cot_own, cot_send = split_halves(sc, cotangent.reshape(128, CH))
        cot_other = swap(cot_send, "d0")
        ids4 = jnp.concatenate([ids_own, swap(ids_own, "d0")], axis=0)
        strips = tile_ring(make_strips(feat_own, feat_other))
        x3 = pad_tiles(sc, ids4, feat_own, feat_other, strips)
        bnd = lax.all_gather(swap(tail, "d0"), lows)[-1]
        arrays = [lax.all_gather(half0, lows), lax.all_gather(half1, lows), bnd]
        plan = [("all", 0, 0, 0), ("all", 0, 1, 0), ("tail", 0, 0, 0)]
    w, hidden, sums = weight_forward(sizes, sc, plan, arrays, x3)
    hidden, cot_other = tie(hidden, cot_other)
    cot, sums = regroup(cot_own, cot_other, hidden, sums)
    sums = sums + swap(sums, "t1")
    cross = [(0, 3), (1, 2), (2, 1), (3, 0)]
    sums = [sums, swap(sums, "t0"), swap(sums, "d0"), lax.ppermute(sums, ("d0", "t0"), cross)]
    gate, fin = gate_stage(sc, sums, squeeze_weight, excite_weight.T)

    out_own, out_send = output_stage(hidden, x3, gate)
    out_send, gate, fin = tie(out_send, gate, fin)
    out_other = swap(out_send, "d0")
    for name in lows[:0:-1]:
        fin = grow(fin, name)
    inner, r0, grad = input_grad(ids4, hidden, cot, gate, w)
    r0, grad, out_other, fin = tie(r0, grad, out_other, fin)
    r2, r1 = swap(r0, "t0"), swap(r0, "t1")
    keep, send, ext = weight_grad(sizes, sc, grad, x3)

    send, ext, r1, r2 = tie(send, ext, r1, r2)
    got = swap(send, "t1")
    ext_near = swap(ext, "d0")
    ext_far = lax.ppermute(ext, ("d0", "t1"), cross)
    r3 = swap(r2, "t1")
    got, ext_near, ext_far, keep = tie(got, ext_near, ext_far, keep)
    ext = ext_near + ext_far
    place = jnp.logical_and(jnp.arange(dl_num)[:, None] == dl ^ (dl_num - 1), jnp.arange(2)[None] == 1 - y)
    place = jnp.logical_and(place, jnp.logical_and(dh == 0, c == 1))
    ext = jnp.where(place[:, :, None, None], ext[None, None], 0.0)
    ext = jnp.pad(ext, ((0, 0), (0, 0), (sizes.quarter - sizes.top, 0), (0, 0)))
    total = keep.astype(F32) + got.astype(F32) + ext
    axes = lows + ("t0",)
    total = total.reshape((2,) * len(axes) + (sizes.quarter, 128))
    most = sizes.quarter * 13 // 32 // 16 * 16
    cuts = [(0, most), (most, 2 * most), (2 * most, sizes.quarter)]
    far = lows[::-1]
    turns = [("t0",) + far, far[:1] + ("t0",) + far[1:], far[-1:] + far[:-1] + ("t0",)]
    state = [(total[..., lo:hi, :], list(axes)) for lo, hi in cuts]
    for step in range(len(axes)):
        halves = [halve(cur, names, turn[step]) for (cur, names), turn in zip(state, turns)]
        sends = [h[0] for h in halves]
        if step == 0:
            *sends, r3 = tie(*sends, r3)
        elif step == 1:
            *sends, back_send, fin, out_own = tie(*sends, back_send, fin, out_own)
        else:
            sends = tie(*sends)
        recv = [swap(v, turn[step]) for v, turn in zip(sends, turns)]
        if step == 0:
            back_own, back_send = add_rims(sc, cot_own, cot_other, inner, [r0, r1, r2, r3])
            *recv, back_own, back_send = tie(*recv, back_own, back_send)
        elif step == 1:
            back_other = swap(back_send, "d0")
            fin = grow(fin, lows[0])
            output = join_halves(sc, out_own, out_other)
            *recv, fin, output = tie(*recv, fin, output)
        elif step == 2:
            *recv, back_other = tie(*recv, back_other)
        else:
            recv = tie(*recv)
        state = [(h[1] + r.astype(F32), h[2]) for h, r in zip(halves, recv)]
    body = jnp.concatenate([cur for cur, _ in state], axis=0).astype(BF16)
    body, back_own, fin = tie(body, back_own, fin)
    p2, p1 = swap(body, "t0"), swap(body, "t1")
    grad_in = join_halves(sc, back_own, back_other)
    grad_squeeze, grad_excite = outer_stage(fin, squeeze_weight.shape[1])
    p2, p1, grad_in, grad_squeeze = tie(p2, p1, grad_in, grad_squeeze)
    parts = [body, p1, p2, swap(p2, "t1")]
    grad_conv = place_rows(sizes, sc, parts)
    shape = features.shape
    return (output.reshape(shape), grad_in.reshape(shape), grad_conv, grad_squeeze, grad_excite.T)


def solution(mesh):
    dbits = mesh.shape["dp"].bit_length() - 1
    dnames = tuple(f"d{i}" for i in range(dbits))
    tnames = ("t0", "t1")
    fine = Mesh(mesh.devices.reshape((2,) * (dbits + 2)), dnames + tnames)
    return jax.shard_map(
        functools.partial(shards, dbits),
        mesh=fine,
        in_specs=(
            P(dnames, tnames, None, None, None),
            P(dnames, tnames, None, None, None),
            P(dnames, None),
            P(),
            P(),
            P(dnames, tnames),
            P(dnames, tnames, None),
        ),
        out_specs=(
            P(dnames, tnames, None, None, None),
            P(dnames, tnames, None, None, None),
            P(dnames, None),
            P(),
            P(),
        ),
        check_vma=False,
    )
```

```python
import functools

import jax
import jax.numpy as jnp
from jax import lax
from jax.experimental import pallas as pl
from jax.experimental.pallas import tpu as pltpu
from jax.sharding import Mesh, PartitionSpec as P

CG = 264
HALF = 3 * CG
TAPROWS = 27 * CG
LEAD = 33 * (TAPROWS // 16)
CH = 2 * HALF
F32 = jnp.float32
BF16 = jnp.bfloat16
SWAP = [(0, 1), (1, 0)]
PCH = 64
NCH = 7
OROWS = 16 * PCH * NCH + 8
VMEM = pl.BlockSpec(memory_space=pltpu.VMEM)
SMEM = pl.BlockSpec(memory_space=pltpu.SMEM)
HBM = pl.BlockSpec(memory_space=pltpu.HBM)


def params(mebibytes):
    return pltpu.CompilerParams(vmem_limit_bytes=mebibytes * 1024 * 1024)


def cost(microseconds):
    return pl.CostEstimate(flops=0, bytes_accessed=int(microseconds * 0.05 * 3.6e6), transcendentals=0)


def swap(value, axis):
    return lax.ppermute(value, axis, SWAP)


class Sizes:
    def __init__(self, rows, dl_num):
        self.rows = rows
        self.dl_num = dl_num
        self.bound = rows * dl_num - LEAD
        self.top = -(-self.bound // 16) * 16
        self.half = -(-rows // 64) * 32
        self.second = rows - self.half
        self.quarter = self.half // 2
        self.flat = self.top + 33 * PCH * NCH + 8


def split_body(sc, x_ref, mine_ref, send_ref):
    low = sc[0] == 0
    for slot in range(2):
        x = x_ref[64 * slot : 64 * slot + 64, :]
        x = jnp.where(slot < sc[4], x, jnp.zeros_like(x))
        first, second = x[:, :HALF], x[:, HALF:]
        mine_ref[slot] = jnp.where(low, first, second)
        send_ref[slot] = jnp.where(low, second, first)


def split_halves(sc, x):
    shape = jax.ShapeDtypeStruct((2, 64, HALF), BF16)
    return pl.pallas_call(
        split_body,
        out_shape=(shape, shape),
        in_specs=[SMEM, VMEM],
        out_specs=(VMEM, VMEM),
        compiler_params=params(10),
        cost_estimate=cost(2),
        name="split_halves",
    )(sc, x)


def join_body(sc, a_ref, b_ref, out_ref, wide):
    low = sc[0] == 0
    for slot in range(2):
        a = a_ref[slot].astype(F32)
        b = b_ref[slot].astype(F32)
        live = slot < sc[4]
        first = jnp.where(low, a, b)
        second = jnp.where(low, b, a)
        wide[:, :HALF] = jnp.where(live, first, 0.0)
        wide[:, HALF:] = jnp.where(live, second, 0.0)
        out_ref[64 * slot : 64 * slot + 64, :] = wide[...].astype(BF16)


def join_halves(sc, a, b):
    return pl.pallas_call(
        join_body,
        out_shape=jax.ShapeDtypeStruct((128, CH), BF16),
        in_specs=[SMEM, VMEM, VMEM],
        out_specs=VMEM,
        scratch_shapes=[pltpu.VMEM((64, CH), F32)],
        compiler_params=params(10),
        cost_estimate=cost(2),
        name="join_halves",
    )(sc, a, b)


def strips_body(own_ref, other_ref, out_ref):
    for t in range(4):
        ref = own_ref if t < 2 else other_ref
        x = ref[t % 2].astype(F32)
        cube = x.reshape(8, 8, HALF)
        out = jnp.concatenate([x[:8], x[56:], cube[:, 0, :], cube[:, 7, :]], axis=0)
        out_ref[t] = out.astype(BF16)


def make_strips(own, other):
    return pl.pallas_call(
        strips_body,
        out_shape=jax.ShapeDtypeStruct((4, 32, HALF), BF16),
        in_specs=[VMEM, VMEM],
        out_specs=VMEM,
        compiler_params=params(10),
        cost_estimate=cost(1.9),
        name="make_strips",
    )(own, other)


def pad_body(sc, ids, own_ref, other_ref, s0, s1, s2, s3, x3_ref, strips, pad):
    for rel, ref in enumerate((s0, s1, s2, s3)):
        strips[rel] = ref[...]
    for t in range(4):
        ref = own_ref if t < 2 else other_ref
        x = ref[t % 2].astype(F32)
        for i in range(8):
            pad[1 + i, t, 1:9, :] = x[8 * i : 8 * i + 8]

        def piece(offset, member):
            n = ids[t, offset]
            safe = jnp.maximum(n, 0)
            rel = jnp.bitwise_xor(lax.shift_right_logical(safe, 1), sc[5])
            other = 2 * (t // 2) + jnp.bitwise_and(safe, 1)
            got = strips[rel, other].astype(F32)[8 * member : 8 * member + 8]
            return jnp.where(n >= 0, got, 0.0)

        pad[0, t, 0:1, :] = piece(0, 1)[7:8]
        pad[0, t, 1:9, :] = piece(1, 1)
        pad[0, t, 9:10, :] = piece(2, 1)[0:1]
        left = piece(3, 3)
        right = piece(4, 2)
        for i in range(8):
            pad[1 + i, t, 0:1, :] = left[i : i + 1]
            pad[1 + i, t, 9:10, :] = right[i : i + 1]
        pad[9, t, 0:1, :] = piece(5, 0)[7:8]
        pad[9, t, 1:9, :] = piece(6, 0)
        pad[9, t, 9:10, :] = piece(7, 0)[0:1]
    for i in range(10):
        for dx in range(3):
            row = pad[i, :, dx : dx + 8, :].reshape(32, HALF)
            for g in range(3):
                x3_ref[g, dx, i] = row[:, CG * g : CG * g + CG].astype(BF16)


def pad_tiles(sc, ids, own, other, strips):
    return pl.pallas_call(
        pad_body,
        out_shape=jax.ShapeDtypeStruct((3, 3, 10, 32, CG), BF16),
        in_specs=[SMEM, SMEM] + [VMEM] * 6,
        out_specs=VMEM,
        scratch_shapes=[
            pltpu.VMEM((4, 4, 32, HALF), BF16),
            pltpu.VMEM((10, 4, 16, HALF), F32),
        ],
        compiler_params=params(20),
        cost_estimate=cost(3.8),
        name="pad_tiles",
    )(sc, ids, own, other, *strips)


def weight_body(sizes, plan, sc, *refs):
    count = len(plan)
    srcs = refs[:count]
    x3_hbm, w_ref, hid_ref, sums_ref, land, tails, flat, o0, o1, o2, built, x3, sems, more = refs[count:]
    load = pltpu.make_async_copy(x3_hbm, x3, more.at[3])
    copies = []
    for pos, (kind, rel, half, quarter) in enumerate(plan):
        src = srcs[pos]
        pairs = []
        if kind == "all":
            pairs.append((src, land.at[:, half]))
        elif kind == "tail":
            pairs.append((src, tails.at[rel]))
        else:
            dl = jnp.bitwise_xor(sc[1], rel)
            if kind == "own":
                pairs.append((src, land.at[dl, half]))
            elif kind == "half":
                pairs.append((src, land.at[dl, jnp.bitwise_xor(sc[2], half)]))
            else:
                start = pl.multiple_of(jnp.bitwise_xor(sc[3], quarter) * sizes.quarter, 16)
                slot = land.at[dl, jnp.bitwise_xor(sc[2], half), pl.ds(start, sizes.quarter)]
                pairs.append((src.at[pl.ds(0, sizes.quarter)], slot))
                if rel == 2:
                    pairs.append((src.at[pl.ds(sizes.quarter, sizes.top)], tails.at[2 * quarter + half]))
        for src, dst in pairs:
            copies.append(pltpu.make_async_copy(src, dst, sems.at[len(copies)]))
            copies[-1].start()
    load.start()
    for copy in copies:
        copy.wait()
    last = 0 if plan[0][0] == "all" else jnp.bitwise_xor(sc[1], sc[5])
    flat[: sizes.top, :] = tails[last].astype(F32)
    for dl in range(sizes.dl_num):
        start = sizes.top + sizes.rows * dl
        flat[start : start + sizes.half, :] = land[dl, 0].astype(F32)
        start += sizes.second
        flat[start : start + sizes.half, :] = land[dl, 1].astype(F32)
    base = jnp.where(sc[0] == 0, sizes.top, sizes.top - sizes.bound)

    @pl.loop(0, NCH)
    def _(ch):
        start = base + ch * (33 * PCH)
        for k in range(16):
            rows = [flat[pl.ds(start + 2 * k + j, PCH, stride=33), :] for j in range(3)]
            x = jnp.concatenate(rows, axis=1)
            if k:
                x = pltpu.roll(x, 384 - 8 * k, axis=1)
            for col, ref in enumerate((o0, o1, o2)):
                ref[pl.ds(ch * (16 * PCH) + k, PCH, stride=16), :] = x[:, 128 * col : 128 * col + 128]

    off = jnp.where(sc[0] == 0, 0, 8)
    stores = []
    for g in range(3):
        for tap in range(9):
            here = pl.ds(pl.multiple_of(off + CG * (9 * g + tap), 8), CG)
            built[g, tap, :, :128] = o0[here, :].astype(BF16)
            built[g, tap, :, 128:256] = o1[here, :].astype(BF16)
            built[g, tap, :, 256:] = o2[here, :8].astype(BF16)
        stores.append(pltpu.make_async_copy(built.at[g], w_ref.at[g], more.at[g]))
        stores[g].start()
        if g == 0:
            load.wait()
        forward_group(sc, g, x3, built, hid_ref, sums_ref)
    for copy in stores:
        copy.wait()


def forward_group(sc, g, x3, w, hid_ref, sums_ref):
    acc = jnp.zeros((256, CG), F32)
    for dx in range(3):
        for dy in range(3):
            x = x3[g, dx, dy : dy + 8].reshape(256, CG)
            acc += jnp.dot(x, w[g, 3 * dy + dx], preferred_element_type=F32)
    hid_ref[g] = acc
    active = (acc * jax.nn.sigmoid(acc)).astype(BF16).astype(F32)
    sums_ref[g] = jnp.full((8, CG), sc[4].astype(F32), F32)
    slide_sums(active, sums_ref, g, 0)


def slide_sums(value, sums_ref, g, row):
    value = value.reshape(8, 4, 8, CG)
    for slide in range(2):
        part = value[:, 2 * slide] + value[:, 2 * slide + 1]
        sums_ref[g, row + slide : row + slide + 1, :] = jnp.sum(jnp.sum(part, axis=0), axis=0, keepdims=True)


def weight_forward(sizes, sc, plan, arrays, x3):
    return pl.pallas_call(
        functools.partial(weight_body, sizes, plan),
        out_shape=(
            jax.ShapeDtypeStruct((3, 9, CG, CG), BF16),
            jax.ShapeDtypeStruct((3, 256, CG), F32),
            jax.ShapeDtypeStruct((3, 8, CG), F32),
        ),
        in_specs=[SMEM] + [HBM] * (len(plan) + 1),
        out_specs=(HBM, VMEM, VMEM),
        scratch_shapes=[
            pltpu.VMEM((sizes.dl_num, 2, sizes.half, 128), BF16),
            pltpu.VMEM((4, sizes.top, 128), BF16),
            pltpu.VMEM((sizes.flat, 128), F32),
            pltpu.VMEM((OROWS, 128), F32),
            pltpu.VMEM((OROWS, 128), F32),
            pltpu.VMEM((OROWS, 128), F32),
            pltpu.VMEM((3, 9, CG, CG), BF16),
            pltpu.VMEM((3, 3, 10, 32, CG), BF16),
            pltpu.SemaphoreType.DMA((len(plan) + 4,)),
            pltpu.SemaphoreType.DMA((4,)),
        ],
        compiler_params=params(48),
        cost_estimate=cost(18),
        name="weight_forward",
    )(sc, *arrays, x3)


def regroup_body(own_ref, other_ref, hid_ref, half_ref, out_ref, sums_ref, cot):
    x = [(own_ref if t < 2 else other_ref)[t % 2].astype(F32) for t in range(4)]
    for i in range(8):
        row = jnp.concatenate([x[t][8 * i : 8 * i + 8] for t in range(4)], axis=0)
        for g in range(3):
            part = row[:, CG * g : CG * g + CG]
            out_ref[g, 32 * i : 32 * i + 32, :] = part.astype(BF16)
            cot[g, 32 * i : 32 * i + 32, :] = part
    for g in range(3):
        hidden = hid_ref[g]
        active = (hidden * jax.nn.sigmoid(hidden)).astype(BF16).astype(F32)
        sums_ref[g] = half_ref[g]
        slide_sums(active * cot[g], sums_ref, g, 2)


def regroup(own, other, hidden, sums):
    return pl.pallas_call(
        regroup_body,
        out_shape=(
            jax.ShapeDtypeStruct((3, 256, CG), BF16),
            jax.ShapeDtypeStruct((3, 8, CG), F32),
        ),
        in_specs=[VMEM] * 4,
        out_specs=(VMEM, VMEM),
        scratch_shapes=[pltpu.VMEM((3, 256, CG), F32)],
        compiler_params=params(12),
        cost_estimate=cost(3.3),
        name="regroup",
    )(own, other, hidden, sums)


def thirds(x):
    hi = x.astype(BF16).astype(F32)
    mid = (x - hi).astype(BF16).astype(F32)
    low = (x - hi - mid).astype(BF16).astype(F32)
    return hi, mid, low


def exact_dot(x, w, contract):
    parts = jnp.concatenate([*thirds(x), jnp.zeros((10, x.shape[1]), F32)], axis=0).astype(BF16)
    out = lax.dot_general(parts, w, (((1,), (contract,)), ((), ())), preferred_element_type=F32)
    return out[0:2] + out[2:4] + out[4:6]


def gate_body(sc, mine_ref, mine_far_ref, other_ref, other_far_ref, sq_ref, ex_ref, gate_ref, fin_ref, wide):
    low = sc[0] == 0
    for g in range(3):
        a = mine_ref[g] + mine_far_ref[g]
        b = other_ref[g] + other_far_ref[g]
        if g == 0:
            counts = jnp.concatenate([a[4:5, 0:1], b[4:5, 0:1]], axis=0)
        a = a[0:4]
        b = jnp.concatenate([b[1:2], b[0:1], b[3:4], b[2:3]], axis=0)
        wide[0:4, CG * g : CG * g + CG] = jnp.where(low, a, b)
        wide[0:4, HALF + CG * g : HALF + CG * g + CG] = jnp.where(low, b, a)
    total = counts * 64.0
    pooled = wide[0:2, :] / total
    gate = wide[2:4, :]
    w_squeeze = sq_ref[...]
    w_excite = ex_ref[...]
    pre = exact_dot(pooled, w_squeeze, 0)
    sig = jax.nn.sigmoid(pre)
    squeezed = pre * sig
    excite = jax.nn.sigmoid(exact_dot(squeezed, w_excite, 1))
    excite_grad = gate * excite * (1.0 - excite)
    slope = sig * (1.0 + pre * (1.0 - sig))
    squeeze_grad = exact_dot(excite_grad, w_excite, 0) * slope
    pool = exact_dot(squeeze_grad, w_squeeze, 1) / total
    half_e = jnp.where(low, excite[:, :HALF], excite[:, HALF:])
    half_p = jnp.where(low, pool[:, :HALF], pool[:, HALF:])
    for g in range(3):
        gate_ref[g, 0:2, :] = half_e[:, CG * g : CG * g + CG]
        gate_ref[g, 2:4, :] = half_p[:, CG * g : CG * g + CG]

    def ordered(x):
        return jnp.where(low, x, jnp.concatenate([x[1:2], x[0:1]], axis=0))

    fin_ref[...] = jnp.zeros_like(fin_ref)
    fin_ref[:, 0:CH] = ordered(pooled)
    fin_ref[:, 1664 : 1664 + CH] = ordered(excite_grad)
    width = squeezed.shape[1]
    fin_ref[:, 3328 : 3328 + width] = ordered(squeezed)
    fin_ref[:, 3712 : 3712 + width] = ordered(squeeze_grad)


def gate_stage(sc, sums, w_squeeze, w_excite):
    return pl.pallas_call(
        gate_body,
        out_shape=(
            jax.ShapeDtypeStruct((3, 8, CG), F32),
            jax.ShapeDtypeStruct((2, 4096), F32),
        ),
        in_specs=[SMEM] + [VMEM] * 6,
        out_specs=(VMEM, VMEM),
        scratch_shapes=[pltpu.VMEM((8, CH), F32)],
        compiler_params=params(16),
        cost_estimate=cost(3.9),
        name="gate_stage",
    )(sc, *sums, w_squeeze, w_excite)


def outer_dot(a, b):
    ah, am, al = thirds(a)
    bh, bm, bl = thirds(b)
    left = jnp.concatenate([ah, ah, ah, am, am, al], axis=0).astype(BF16)
    right = jnp.concatenate([bh, bm, bl, bh, bm, bh], axis=0).astype(BF16)
    return lax.dot_general(left, right, (((0,), (0,)), ((), ())), preferred_element_type=F32)


def outer_body(width, fin_ref, sq_ref, ex_ref):
    pooled = fin_ref[:, 0:CH]
    excite_grad = fin_ref[:, 1664 : 1664 + CH]
    squeezed = fin_ref[:, 3328 : 3328 + width]
    squeeze_grad = fin_ref[:, 3712 : 3712 + width]
    sq_ref[...] = outer_dot(pooled, squeeze_grad)
    ex_ref[...] = outer_dot(excite_grad, squeezed)


def outer_stage(fin, width):
    return pl.pallas_call(
        functools.partial(outer_body, width),
        out_shape=(
            jax.ShapeDtypeStruct((CH, width), F32),
            jax.ShapeDtypeStruct((CH, width), F32),
        ),
        in_specs=[VMEM],
        out_specs=(VMEM, VMEM),
        compiler_params=params(20),
        cost_estimate=cost(3.7),
        name="outer_stage",
    )(fin)


def output_body(hid_ref, x3_ref, gate_ref, own_ref, other_ref, wide):
    for g in range(3):
        gate = gate_ref[g]
        by_slide = jnp.concatenate(
            [jnp.broadcast_to(gate[s : s + 1], (16, CG)) for s in range(2)], axis=0
        )
        for i in range(8):
            hidden = hid_ref[g, 32 * i : 32 * i + 32, :]
            active = (hidden * jax.nn.sigmoid(hidden)).astype(BF16).astype(F32)
            value = x3_ref[g, 1, 1 + i].astype(F32) + active * by_slide
            for t in range(4):
                wide[t, 8 * i : 8 * i + 8, CG * g : CG * g + CG] = value[8 * t : 8 * t + 8]
    for t in range(4):
        (own_ref if t < 2 else other_ref)[t % 2] = wide[t].astype(BF16)


def output_stage(hidden, x3, gate):
    shape = jax.ShapeDtypeStruct((2, 64, HALF), BF16)
    return pl.pallas_call(
        output_body,
        out_shape=(shape, shape),
        in_specs=[VMEM] * 3,
        out_specs=(VMEM, VMEM),
        scratch_shapes=[pltpu.VMEM((4, 64, HALF), F32)],
        compiler_params=params(16),
        cost_estimate=cost(3.1),
        name="output_stage",
    )(hidden, x3, gate)


def hidden_slope(hid_ref, cot_ref, gate_ref):
    hidden = hid_ref[0]
    gate = gate_ref[0]

    def spread(row):
        pair = [jnp.broadcast_to(gate[row + s : row + s + 1], (16, CG)) for s in range(2)]
        both = jnp.concatenate(pair, axis=0)
        return jnp.broadcast_to(both[None], (8, 32, CG)).reshape(256, CG)

    sig = jax.nn.sigmoid(hidden)
    slope = sig * (1.0 + hidden * (1.0 - sig))
    return ((cot_ref[0].astype(F32) * spread(0) + spread(2)) * slope).astype(BF16)


def weight_grad_body(sizes, sc, grad_ref, x3_ref, keep_ref, send_ref, ext_ref, flat, carry):
    g = pl.program_id(0)

    @pl.when(g == 0)
    def _():
        end = sizes.top + sizes.rows * sizes.dl_num
        flat[: sizes.top, :] = jnp.zeros((sizes.top, 128), F32)
        flat[end - 16 : end, :] = jnp.zeros((16, 128), F32)
        carry[...] = jnp.zeros_like(carry)

    grad = grad_ref[0]
    base = jnp.where(sc[0] == 0, sizes.top, sizes.top - sizes.bound)
    first = jnp.where(sc[0] == 0, 0, 1) + g * (9 * 33)
    row = lax.broadcasted_iota(jnp.int32, (8, 128), 0)
    lane = lax.broadcasted_iota(jnp.int32, (8, 128), 1)
    edge = lane - 8 * row
    zeros = jnp.zeros((CG, 120), F32)

    def taps(odd):
        held = carry[...]
        for tap in range(9):
            dy, dx = divmod(tap, 3)
            x = x3_ref[0, dx, dy : dy + 8].reshape(256, CG)
            res = lax.dot_general(x, grad, (((0,), (0,)), ((), ())), preferred_element_type=F32)
            res = jnp.concatenate([res, zeros], axis=1)
            for i in range(33):
                h = (odd + tap + i) % 2
                place = first + 33 * tap + i
                start = base + 33 * lax.shift_right_logical(place, 1) + 16 * h
                turned = [
                    pltpu.roll(
                        res[8 * i : 8 * i + 8, 128 * col : 128 * col + 128], 64 * h, axis=1, stride=8, stride_axis=0
                    )
                    for col in range(3)
                ]
                own = edge >= 64 * h
                third = jnp.where(own, turned[2], turned[1])
                shifted = pltpu.roll(third, 1, axis=0)
                before = jnp.where(row == 0, held, shifted)
                flat[pl.ds(start, 8, stride=2), :] = jnp.where(own, turned[0], before)
                flat[pl.ds(start + 1, 8, stride=2), :] = jnp.where(own, turned[1], turned[0])
                flat[pl.ds(start + 16, 1), :] = third[7:8]
                held = shifted
        carry[...] = held

    parity = jnp.bitwise_and(first, 1)
    for odd in range(2):
        @pl.when(parity == odd)
        def _():
            taps(odd)

    @pl.when(g == 2)
    def _():
        even = sc[2] == 0
        quarter = sizes.quarter
        ext_ref[...] = flat[: sizes.top, :]
        for dl in range(sizes.dl_num):
            for q in range(2):
                start = sizes.top + sizes.rows * dl + q * quarter
                v0 = flat[start : start + quarter, :]
                v1 = flat[start + sizes.second : start + sizes.second + quarter, :]
                rel = jnp.bitwise_xor(sc[1], dl)
                part = jnp.bitwise_xor(sc[3], q)
                keep_ref[rel, part] = jnp.where(even, v0, v1).astype(BF16)
                send_ref[rel, part] = jnp.where(even, v1, v0).astype(BF16)


def weight_grad(sizes, sc, grad, x3):
    pieces = jax.ShapeDtypeStruct((sizes.dl_num, 2, sizes.quarter, 128), BF16)
    return pl.pallas_call(
        functools.partial(weight_grad_body, sizes),
        grid=(3,),
        out_shape=(
            pieces,
            pieces,
            jax.ShapeDtypeStruct((sizes.top, 128), F32),
        ),
        in_specs=[
            SMEM,
            pl.BlockSpec((1, 256, CG), lambda g: (g, 0, 0)),
            pl.BlockSpec((1, 3, 10, 32, CG), lambda g: (g, 0, 0, 0, 0)),
        ],
        out_specs=(VMEM, VMEM, VMEM),
        scratch_shapes=[
            pltpu.VMEM((sizes.flat, 128), F32),
            pltpu.VMEM((8, 128), F32),
        ],
        compiler_params=params(32),
        cost_estimate=cost(11.9),
        name="weight_grad",
    )(sc, grad, x3)


def input_grad_body(ids, hid_ref, cot_ref, gate_ref, w_ref, inner_ref, rim_ref, grad_ref, pads, part, cols, w, sems):
    g = pl.program_id(0)


    @pl.when(g == 0)
    def _():
        for group in range(3):
            pltpu.make_async_copy(w_ref.at[group], w.at[group], sems.at[group]).start()

    part[...] = jnp.zeros_like(part)
    grad = hidden_slope(hid_ref, cot_ref, gate_ref)
    grad_ref[0] = grad
    pltpu.make_async_copy(w_ref.at[g], w.at[g], sems.at[g]).wait()
    for dx in range(3):
        cols[...] = jnp.zeros_like(cols)
        for dy in range(3):
            d = lax.dot_general(grad, w[g, 3 * dy + dx], (((1,), (1,)), ((), ())), preferred_element_type=F32)
            cols[dy : dy + 8] += d.reshape(8, 32, CG)
        part[:, :, dx : dx + 8, :] += cols[...].reshape(10, 4, 8, CG)
    for value in range(3):
        @pl.when(g == value)
        def _():
            pads[:, :, :, CG * value : CG * value + CG] = part[...]

    @pl.when(g == 2)
    def _():
        for t in range(4):
            for i in range(8):
                inner_ref[t, 8 * i : 8 * i + 8, :] = pads[1 + i, t, 1:9, :]
            left = jnp.concatenate([pads[1 + i, t, 0:1, :] for i in range(8)], axis=0)
            right = jnp.concatenate([pads[1 + i, t, 9:10, :] for i in range(8)], axis=0)
            corners = [pads[0, t, 0:1, :], pads[0, t, 9:10, :], pads[9, t, 0:1, :], pads[9, t, 9:10, :]]
            lane = lax.broadcasted_iota(jnp.int32, (4, HALF), 1)
            listed = jnp.full((4, HALF), -1.0, F32)
            for k in range(8):
                listed = jnp.where(lane == k, ids[t, k].astype(F32), listed)
            parts = [pads[0, t, 1:9, :], left, right, pads[9, t, 1:9, :], *corners, listed]
            rim_ref[t] = jnp.concatenate(parts, axis=0).astype(BF16)


def input_grad(ids, hidden, cot, gate, w):
    return pl.pallas_call(
        input_grad_body,
        grid=(3,),
        out_shape=(
            jax.ShapeDtypeStruct((4, 64, HALF), F32),
            jax.ShapeDtypeStruct((4, 40, HALF), BF16),
            jax.ShapeDtypeStruct((3, 256, CG), BF16),
        ),
        in_specs=[
            SMEM,
            pl.BlockSpec((1, 256, CG), lambda g: (g, 0, 0)),
            pl.BlockSpec((1, 256, CG), lambda g: (g, 0, 0)),
            pl.BlockSpec((1, 8, CG), lambda g: (g, 0, 0)),
            HBM,
        ],
        out_specs=(VMEM, VMEM, pl.BlockSpec((1, 256, CG), lambda g: (g, 0, 0))),
        scratch_shapes=[
            pltpu.VMEM((10, 4, 16, HALF), F32),
            pltpu.VMEM((10, 4, 16, CG), F32),
            pltpu.VMEM((10, 32, CG), F32),
            pltpu.VMEM((3, 9, CG, CG), BF16),
            pltpu.SemaphoreType.DMA((3,)),
        ],
        compiler_params=params(28),
        cost_estimate=cost(9.5),
        name="input_grad",
    )(ids, hidden, cot, gate, w)


def rims_body(sc, own_ref, other_ref, inner_ref, r0, r1, r2, r3, out0_ref, out1_ref, edges, corners):
    edges[...] = jnp.zeros_like(edges)
    corners[...] = jnp.zeros_like(corners)
    for ref in (r0, r1, r2, r3):
        for slide in range(2):
            for slot in range(2):
                t = 2 * slide + slot
                rim = ref[t].astype(F32)
                for mine in range(2):
                    own = (2 * sc[5] + mine).astype(F32)
                    n = 2 * slide + mine

                    def hit(offset):
                        return jnp.where(rim[36:37, offset : offset + 1] == own, 1.0, 0.0)

                    for member, offset in enumerate((1, 3, 4, 6)):
                        edges[n, member] += hit(offset) * rim[8 * member : 8 * member + 8]
                    for member, offset in enumerate((0, 2, 5, 7)):
                        row = 32 + member
                        corners[n, member : member + 1] += hit(offset) * rim[row : row + 1]
    for n in range(4):
        cot = (own_ref if n < 2 else other_ref)[n % 2].astype(F32)
        inner_ref_n = inner_ref[n] + cot
        last_col = edges[n, 1]
        first_col = edges[n, 2]
        rows = []
        for i in range(8):
            row = inner_ref_n[8 * i : 8 * i + 8]
            lo = first_col[i : i + 1]
            hi = last_col[i : i + 1]
            if i == 0:
                row = row + edges[n, 3]
                hi = hi + corners[n, 2:3]
                lo = lo + corners[n, 3:4]
            if i == 7:
                row = row + edges[n, 0]
                hi = hi + corners[n, 0:1]
                lo = lo + corners[n, 1:2]
            pos = lax.broadcasted_iota(jnp.int32, (8, HALF), 0)
            row = row + jnp.where(pos == 0, lo, 0.0) + jnp.where(pos == 7, hi, 0.0)
            rows.append(row)
        (out0_ref if n < 2 else out1_ref)[n % 2] = jnp.concatenate(rows, axis=0).astype(BF16)


def add_rims(sc, own, other, inner, rims):
    shape = jax.ShapeDtypeStruct((2, 64, HALF), BF16)
    return pl.pallas_call(
        rims_body,
        out_shape=(shape, shape),
        in_specs=[SMEM] + [VMEM] * 7,
        out_specs=(VMEM, VMEM),
        scratch_shapes=[
            pltpu.VMEM((4, 4, 8, HALF), F32),
            pltpu.VMEM((4, 8, HALF), F32),
        ],
        compiler_params=params(16),
        cost_estimate=cost(3.4),
        name="add_rims",
    )(sc, own, other, inner, *rims)


def rows_body(sizes, sc, p0, p1, p2, p3, out_ref, land, sems):
    copies = []
    for rel, ref in enumerate((p0, p1, p2, p3)):
        c = jnp.bitwise_xor(sc[2], rel & 1)
        q = jnp.bitwise_xor(sc[3], rel >> 1)
        copies.append(pltpu.make_async_copy(ref, land.at[c, q], sems.at[rel]))
        copies[-1].start()
    for copy in copies:
        copy.wait()
    for c in range(2):
        for q in range(2):
            start = c * sizes.second + q * sizes.quarter
            out_ref[start : start + sizes.quarter, :] = land[c, q].astype(F32)


def place_rows(sizes, sc, parts):
    return pl.pallas_call(
        functools.partial(rows_body, sizes),
        out_shape=jax.ShapeDtypeStruct((sizes.rows, 128), F32),
        in_specs=[SMEM] + [HBM] * 4,
        out_specs=VMEM,
        scratch_shapes=[
            pltpu.VMEM((2, 2, sizes.quarter, 128), BF16),
            pltpu.SemaphoreType.DMA((4,)),
        ],
        compiler_params=params(12),
        cost_estimate=cost(3),
        name="place_rows",
    )(sc, *parts)


def tile_ring(value):
    near = swap(value, "t1")
    far = swap(value, "t0")
    return value, near, far, swap(far, "t1")


def tie(*values):
    return lax.optimization_barrier(values)


def grow(value, name):
    other = swap(value, name)
    first = lax.axis_index(name) == 0
    return jnp.concatenate([jnp.where(first, value, other), jnp.where(first, other, value)], axis=0)


def halve(current, names, name):
    pos = names.index(name)
    send = lax.index_in_dim(current, 1, pos, keepdims=False).astype(BF16)
    stay = lax.index_in_dim(current, 0, pos, keepdims=False)
    return send, stay, [n for n in names if n != name]


def shards(dbits, features, cotangent, conv_weight, squeeze_weight, excite_weight, live_count, neighbours):
    lows = tuple(f"d{i}" for i in range(1, dbits))
    dl_num = 2 ** (dbits - 1)
    sizes = Sizes(conv_weight.shape[0], dl_num)
    dh = lax.axis_index("d0")
    dl = lax.axis_index(lows)
    y = lax.axis_index("t0")
    c = lax.axis_index("t1")
    count = live_count[0, 0]
    sc = jnp.stack([dh, dl, c, y, count, 2 * y + c, count, count]).astype(jnp.int32)

    half0 = conv_weight[: sizes.half]
    half1 = conv_weight[sizes.second :]
    tail = conv_weight[sizes.rows - sizes.top :]
    ids_own = neighbours[0]
    if len(lows) == 2:
        mine = jnp.where(c == 0, half0, half1)
        part = jnp.where(y == 0, mine[: sizes.quarter], mine[sizes.quarter :])
        mine, part, features = tie(mine, part, features)
        a2 = swap(mine, "d2")
        q1 = swap(part, "d1")
        bnd = lax.ppermute(tail, ("d0",) + lows + ("t0", "t1"), [(12 + t, 16 + 5 * t) for t in range(4)])
        feat_own, feat_send = split_halves(sc, features.reshape(128, CH))
        feat_other = swap(feat_send, "d0")
        ids4 = jnp.concatenate([ids_own, swap(ids_own, "d0")], axis=0)
        s0 = make_strips(feat_own, feat_other)
        q1, feat_own = tie(q1, feat_own)
        q3 = swap(q1, "d2")
        q1 = jnp.concatenate([q1, bnd], axis=0)
        y1 = swap(q1, "t0")
        s0, y1, q3, ids4, cotangent = tie(s0, y1, q3, ids4, cotangent)
        cot_own, cot_send = split_halves(sc, cotangent.reshape(128, CH))
        s1, s2 = swap(s0, "t1"), swap(s0, "t0")
        s1, s2, q3, y1, cot_send = tie(s1, s2, q3, y1, cot_send)
        y3 = swap(q3, "t0")
        cot_other = swap(cot_send, "d0")
        strips = [s0, s1, s2, swap(s2, "t1")]
        near = [swap(p, "t1") for p in (a2, q1, q3, y1)]
        x3 = pad_tiles(sc, ids4, feat_own, feat_other, strips)
        y3, x3 = tie(y3, x3)
        arrays = [bnd, half0, half1, a2, q1, q3, y1, y3, *near, swap(y3, "t1")]
        plan = [("tail", 0, 0, 0), ("own", 0, 0, 0), ("own", 0, 1, 0)]
        for half in range(2):
            plan += [("half", 1, half, 0), ("quarter", 2, half, 0), ("quarter", 3, half, 0),
                     ("quarter", 2, half, 1), ("quarter", 3, half, 1)]
    else:
        feat_own, feat_send = split_halves(sc, features.reshape(128, CH))
        feat_other = swap(feat_send, "d0")
        cot_own, cot_send = split_halves(sc, cotangent.reshape(128, CH))
        cot_other = swap(cot_send, "d0")
        ids4 = jnp.concatenate([ids_own, swap(ids_own, "d0")], axis=0)
        strips = tile_ring(make_strips(feat_own, feat_other))
        x3 = pad_tiles(sc, ids4, feat_own, feat_other, strips)
        bnd = lax.all_gather(swap(tail, "d0"), lows)[-1]
        arrays = [lax.all_gather(half0, lows), lax.all_gather(half1, lows), bnd]
        plan = [("all", 0, 0, 0), ("all", 0, 1, 0), ("tail", 0, 0, 0)]
    w, hidden, sums = weight_forward(sizes, sc, plan, arrays, x3)
    hidden, cot_other = tie(hidden, cot_other)
    cot, sums = regroup(cot_own, cot_other, hidden, sums)
    sums = sums + swap(sums, "t1")
    cross = [(0, 3), (1, 2), (2, 1), (3, 0)]
    sums = [sums, swap(sums, "t0"), swap(sums, "d0"), lax.ppermute(sums, ("d0", "t0"), cross)]
    gate, fin = gate_stage(sc, sums, squeeze_weight, excite_weight.T)

    out_own, out_send = output_stage(hidden, x3, gate)
    out_send, gate, fin = tie(out_send, gate, fin)
    out_other = swap(out_send, "d0")
    for name in lows[:0:-1]:
        fin = grow(fin, name)
    inner, r0, grad = input_grad(ids4, hidden, cot, gate, w)
    r0, grad, out_other, fin = tie(r0, grad, out_other, fin)
    r2, r1 = swap(r0, "t0"), swap(r0, "t1")
    keep, send, ext = weight_grad(sizes, sc, grad, x3)

    send, ext, r1, r2 = tie(send, ext, r1, r2)
    got = swap(send, "t1")
    ext_near = swap(ext, "d0")
    ext_far = lax.ppermute(ext, ("d0", "t1"), cross)
    r3 = swap(r2, "t1")
    got, ext_near, ext_far, keep = tie(got, ext_near, ext_far, keep)
    ext = ext_near + ext_far
    place = jnp.logical_and(jnp.arange(dl_num)[:, None] == dl ^ (dl_num - 1), jnp.arange(2)[None] == 1 - y)
    place = jnp.logical_and(place, jnp.logical_and(dh == 0, c == 1))
    ext = jnp.where(place[:, :, None, None], ext[None, None], 0.0)
    ext = jnp.pad(ext, ((0, 0), (0, 0), (sizes.quarter - sizes.top, 0), (0, 0)))
    total = keep.astype(F32) + got.astype(F32) + ext
    axes = lows + ("t0",)
    total = total.reshape((2,) * len(axes) + (sizes.quarter, 128))
    most = sizes.quarter * 13 // 32 // 16 * 16
    cuts = [(0, most), (most, 2 * most), (2 * most, sizes.quarter)]
    far = lows[::-1]
    turns = [("t0",) + far, far[:1] + ("t0",) + far[1:], far[-1:] + far[:-1] + ("t0",)]
    state = [(total[..., lo:hi, :], list(axes)) for lo, hi in cuts]
    for step in range(len(axes)):
        halves = [halve(cur, names, turn[step]) for (cur, names), turn in zip(state, turns)]
        sends = [h[0] for h in halves]
        if step == 0:
            *sends, r3 = tie(*sends, r3)
        elif step == 1:
            *sends, back_send, fin, out_own = tie(*sends, back_send, fin, out_own)
        else:
            sends = tie(*sends)
        recv = [swap(v, turn[step]) for v, turn in zip(sends, turns)]
        if step == 0:
            back_own, back_send = add_rims(sc, cot_own, cot_other, inner, [r0, r1, r2, r3])
            *recv, back_own, back_send = tie(*recv, back_own, back_send)
        elif step == 1:
            back_other = swap(back_send, "d0")
            fin = grow(fin, lows[0])
            output = join_halves(sc, out_own, out_other)
            *recv, fin, output = tie(*recv, fin, output)
        elif step == 2:
            *recv, back_other = tie(*recv, back_other)
        else:
            recv = tie(*recv)
        state = [(h[1] + r.astype(F32), h[2]) for h, r in zip(halves, recv)]
    body = jnp.concatenate([cur for cur, _ in state], axis=0).astype(BF16)
    body, back_own, fin = tie(body, back_own, fin)
    p2, p1 = swap(body, "t0"), swap(body, "t1")
    grad_in = join_halves(sc, back_own, back_other)
    grad_squeeze, grad_excite = outer_stage(fin, squeeze_weight.shape[1])
    p2, p1, grad_in, grad_squeeze = tie(p2, p1, grad_in, grad_squeeze)
    parts = [body, p1, p2, swap(p2, "t1")]
    grad_conv = place_rows(sizes, sc, parts)
    shape = features.shape
    return (output.reshape(shape), grad_in.reshape(shape), grad_conv, grad_squeeze, grad_excite.T)


def solution(mesh):
    dbits = mesh.shape["dp"].bit_length() - 1
    dnames = tuple(f"d{i}" for i in range(dbits))
    tnames = ("t0", "t1")
    fine = Mesh(mesh.devices.reshape((2,) * (dbits + 2)), dnames + tnames)
    return jax.shard_map(
        functools.partial(shards, dbits),
        mesh=fine,
        in_specs=(
            P(dnames, tnames, None, None, None),
            P(dnames, tnames, None, None, None),
            P(dnames, None),
            P(),
            P(),
            P(dnames, tnames),
            P(dnames, tnames, None),
        ),
        out_specs=(
            P(dnames, tnames, None, None, None),
            P(dnames, tnames, None, None, None),
            P(dnames, None),
            P(),
            P(),
        ),
        check_vma=False,
    )
```
